128 devices in a mesh: grp: 4 (over y), usr: 32 (over z, x, core).
Axes of the slice: x: 4, y: 4, z: 4, core: 2. Of those that a mesh axis runs over, the one named last changes fastest.
Arguments:
- item_factors: bfloat16 [4, 1024, 128, 256], P('grp', 'usr'), may hold values from -0.29882812 to 0.29882812
- send_ids: int32 [4, 32, 32, 3], P('grp', 'usr'), may hold values from 0 to 31, as said below
- send_count: int32 [4, 32, 32], P('grp', 'usr'), may hold values from 0 to 3
- rating_pointer: int32 [4, 1792, 768], P('grp', 'usr'), may hold values from 0 to 12287
- rating_centred_value: bfloat16 [4, 1792, 768], P('grp', 'usr'), may hold values from -6 to 6
- noise: float32 [1792, 256], P('usr'), may hold values from -6 to 6
- prior_prec: float32 [256, 256], replicated, as said below
- prior_shift: float32 [256], replicated, may hold values from -6 to 6
Outputs:
- user_factors: float32 [1792, 256], P('usr')
- item_stats: float32 [4, 1024, 128, 256], P('grp', 'usr')
The draws below stay inside these ranges and needn't reach their ends.
Inputs may be any that keep to these rules, and one draw needn't show every extreme that they name: `send_ids`: the 3 block ids of one list are distinct. `prior_prec`: symmetric with a positive diagonal larger than the sum of the magnitudes of the rest of its row.
All inputs are finite; a program needn't handle non-finite values.
Results may differ from the reference program's by a relative error of at most 0.0003.
Values may be sent and summed in bfloat16 or wider, within the bound.
A program may use at most 192 MiB of HBM per device.

```python
import jax
import jax.numpy as jnp
from jax import lax

K = 256
ITEMS_PER_BLOCK = 128
MAX_BLOCKS_SENT = 3
U_DEV = 56
RATINGS_PER_USER = 768
BLK_DEV = 32
TOTAL_USERS = 1792
ITEM_BLOCKS = 1024
N_GRP = 4
N_USR = 32


def draw_send_ids(key, part):
    key = jax.random.fold_in(key, 11)
    scores = jax.random.randint(key, (N_GRP, N_USR, N_USR, BLK_DEV), 0, 1 << 20) * BLK_DEV
    scores = scores + jnp.arange(BLK_DEV, dtype=jnp.int32)
    order = jnp.argsort(scores, axis=-1, stable=True)
    return order[..., :MAX_BLOCKS_SENT].astype(jnp.int32)


def draw_send_count(key, part):
    key = jax.random.fold_in(key, 12)
    first, second, third = jax.random.split(key, 3)
    heavy = jax.random.randint(first, (N_GRP, N_USR, 1), 1, MAX_BLOCKS_SENT + 1)
    base = jax.random.randint(second, (N_GRP, N_USR, N_USR), 0, MAX_BLOCKS_SENT + 1)
    counts = jnp.minimum(base, heavy)
    target = jax.random.randint(third, (N_GRP, 1, 1), 0, N_USR)
    column = jnp.arange(N_USR, dtype=jnp.int32)[None, None, :]
    return jnp.where(column == target, MAX_BLOCKS_SENT, counts).astype(jnp.int32)


def draw_prior_prec(key, part):
    key = jax.random.fold_in(key, 13)
    first, second = jax.random.split(key)
    spread = jax.random.uniform(first, (K, K), jnp.float32, -1.0, 1.0) / K
    sym = (spread + spread.T) * 0.5
    diag = jax.random.uniform(second, (K,), jnp.float32, 1.0, 2.0)
    ident = (jnp.arange(K)[:, None] == jnp.arange(K)[None, :]).astype(jnp.float32)
    return (sym * (1.0 - ident) + ident * diag[None, :]).astype(jnp.float32)


def touch_ends(array, stream_key, smallest, top_value):
    extent = array.shape
    index_at = [jax.random.randint(jax.random.fold_in(stream_key, axis), (), 0, extent[axis]) for axis in range(len(extent))]
    array = array.at[tuple(index_at)].set(smallest)
    longest = extent.index(max(extent))
    index_at[longest] = (index_at[longest] + 1) % extent[longest]
    return array.at[tuple(index_at)].set(top_value)


def block_scale(own_key, shape, cuts, smallest, largest):
    level, own = 1.0, jax.random.fold_in(own_key, 6)
    for dim, blocks in cuts:
        heights = jnp.exp(jax.random.uniform(jax.random.fold_in(own, dim), (blocks,), jnp.float32, smallest / len(cuts), largest / len(cuts)))
        level = level * jnp.repeat(heights, shape[dim] // blocks).reshape([-1 if axis == dim else 1 for axis in range(len(shape))])
    return level


def normal_values(key, shape, width, limit, shards=(), held_as=jnp.bfloat16):
    level = block_scale(key, shape, shards, -0.22, 0.18) if shards else 1.0
    result = jax.random.normal(key, shape, jnp.float32) * width * level
    return jnp.minimum(jnp.maximum(result, -limit), limit).astype(held_as)


def setup_inputs(seed: int = 0) -> dict:
    arg_keys = jax.random.split(jax.random.key(seed), 9)
    return {
        "item_factors": normal_values(arg_keys[0], (N_GRP, ITEM_BLOCKS, ITEMS_PER_BLOCK, K), 0.05, 0.29882812, ((0, 4), (1, 32))),
        "send_ids": draw_send_ids(jax.random.fold_in(arg_keys[8], 71), 0),
        "send_count": draw_send_count(jax.random.fold_in(arg_keys[8], 71), 0),
        "rating_pointer": touch_ends(jax.random.randint(arg_keys[3], (N_GRP, TOTAL_USERS, RATINGS_PER_USER), 0, N_USR * MAX_BLOCKS_SENT * ITEMS_PER_BLOCK), jax.random.fold_in(arg_keys[3], 1), 0, (N_USR * MAX_BLOCKS_SENT * ITEMS_PER_BLOCK) - 1).astype(jnp.int32),
        "rating_centred_value": normal_values(arg_keys[4], (N_GRP, TOTAL_USERS, RATINGS_PER_USER), 1.0, 6.0, ((0, 4), (1, 32))),
        "noise": normal_values(arg_keys[5], (TOTAL_USERS, K), 1.0, 6.0, ((0, 32),), jnp.float32),
        "prior_prec": draw_prior_prec(jax.random.fold_in(arg_keys[8], 71), 0),
        "prior_shift": normal_values(arg_keys[7], (K,), 1.0, 6.0, (), jnp.float32),
    }


ALPHA = 2.0

def tri_solve(lower, right, transpose):
    return jax.scipy.linalg.solve_triangular(lower, right, lower=True, trans=transpose)

def device_terms(item_factors, send_ids, send_count, rating_pointer, rating_centred_value, group, device):
    refs = lax.dynamic_slice_in_dim(rating_pointer[group], device * U_DEV, U_DEV, 0)
    values = lax.dynamic_slice_in_dim(rating_centred_value[group], device * U_DEV, U_DEV, 0)
    counts = lax.dynamic_index_in_dim(send_count[group], device, 1, keepdims=False)
    listed = lax.dynamic_index_in_dim(send_ids[group], device, 1, keepdims=False)
    source = refs // (MAX_BLOCKS_SENT * ITEMS_PER_BLOCK)
    column = refs // ITEMS_PER_BLOCK % MAX_BLOCKS_SENT
    row_of = refs % ITEMS_PER_BLOCK
    live = column < counts[source]
    block = source * BLK_DEV + listed[source, column]
    rows = item_factors[group][block, row_of]
    masked = jnp.where(live[..., None], rows, jnp.zeros_like(rows))
    live_value = jnp.where(live, values, jnp.zeros_like(values))
    return (masked, live_value, block, row_of)

def reference(item_factors, send_ids, send_count, rating_pointer, rating_centred_value, noise, prior_prec, prior_shift):

    def sample_device(device):
        gram = jnp.zeros((U_DEV, K, K), jnp.float32)
        linear = jnp.zeros((U_DEV, K), jnp.float32)
        for group in range(N_GRP):
            masked, live_value, block, row_of = device_terms(item_factors, send_ids, send_count, rating_pointer, rating_centred_value, group, device)
            masked = masked.astype(jnp.float32)
            gram = gram + jnp.einsum('urk,url->ukl', masked, masked)
            linear = linear + jnp.einsum('ur,urk->uk', live_value.astype(jnp.float32), masked)
        draws = lax.dynamic_slice_in_dim(noise, device * U_DEV, U_DEV, 0)
        lower = jnp.linalg.cholesky(prior_prec[None] + ALPHA * gram)
        inner = tri_solve(lower, (ALPHA * linear + prior_shift[None])[..., None], 0)
        return tri_solve(lower, inner + draws[..., None], 1)[..., 0]
    samples = lax.map(sample_device, jnp.arange(N_USR, dtype=jnp.int32))
    user_factors = samples.reshape(TOTAL_USERS, K)
    stats_list = []
    for group in range(N_GRP):

        def add_device(device, stats):
            masked, live_value, block, row_of = device_terms(item_factors, send_ids, send_count, rating_pointer, rating_centred_value, group, device)
            own = lax.dynamic_index_in_dim(samples, device, 0, keepdims=False)
            terms = (ALPHA * live_value.astype(jnp.float32))[..., None] * own[:, None, :]
            flat = (block * ITEMS_PER_BLOCK + row_of).reshape(-1)
            return stats.at[flat].add(terms.reshape(-1, K))
        stats = lax.fori_loop(0, N_USR, add_device, jnp.zeros((ITEM_BLOCKS * ITEMS_PER_BLOCK, K), jnp.float32))
        stats_list.append(stats.reshape(ITEM_BLOCKS, ITEMS_PER_BLOCK, K))
    return (user_factors, jnp.stack(stats_list, 0))
```

```python
import functools

import jax
import jax.numpy as jnp
from jax import lax
from jax.experimental import pallas as pl
from jax.experimental.pallas import tpu as pltpu
from jax.sharding import PartitionSpec as P

ALPHA = 2.0
F32 = jnp.float32
BF16 = jnp.bfloat16
MIB = 2**20


def iota(shape, dim):
    return lax.broadcasted_iota(jnp.int32, shape, dim)


def split(x):
    hi = x.astype(BF16).astype(F32)
    return hi, x - hi


def stacked(x):
    hi, lo = split(x)
    left = jnp.concatenate([hi, hi, lo, lo], axis=0).astype(BF16)
    right = jnp.concatenate([hi, lo, hi, lo], axis=0).astype(BF16)
    return left, right


def dot_tn(a, b):
    return lax.dot_general(a, b, (((0,), (0,)), ((), ())), preferred_element_type=F32)


def pick_kernel(cols, per_step, listed, live, blocks, out):
    base = pl.program_id(0) * per_step

    def body(i, carry):
        keep = live[base + i] > 0
        block = blocks[listed[base + i]]
        out[i] = jnp.where(keep, block, jnp.zeros_like(block))
        return carry

    lax.fori_loop(0, per_step, body, 0)


def pick_blocks(blocks, listed, live):
    n = listed.shape[0]
    owned, height, rank = blocks.shape
    steps = 4
    per_step = n // steps
    return pl.pallas_call(
        functools.partial(pick_kernel, n, per_step),
        grid_spec=pltpu.PrefetchScalarGridSpec(
            num_scalar_prefetch=2,
            grid=(steps,),
            in_specs=[pl.BlockSpec((owned, height, rank), lambda s, *_: (0, 0, 0))],
            out_specs=pl.BlockSpec((per_step, height, rank), lambda s, *_: (s, 0, 0)),
        ),
        out_shape=jax.ShapeDtypeStruct((n, height, rank), BF16),
        compiler_params=pltpu.CompilerParams(vmem_limit_bytes=32 * MIB),
        name="pick_blocks",
    )(listed, live, blocks)


def weight_kernel(refs, values, out):
    n_blocks, users, height = out.shape
    slots = refs.shape[1]
    for u in range(users):
        ref = refs[u : u + 1, :]
        value = values[u : u + 1, :].astype(F32)
        block = ref // height
        row = ref % height
        hot_block = jnp.where(iota((n_blocks, slots), 0) == block, value, 0.0).astype(BF16)
        hot_row = jnp.where(iota((height, slots), 0) == row, 1.0, 0.0).astype(BF16)
        out[:, u, :] = lax.dot_general(hot_block, hot_row, (((1,), (1,)), ((), ())), preferred_element_type=F32)


def make_weights(refs, values, n_blocks, height):
    users, slots = refs.shape
    group = 8
    return pl.pallas_call(
        weight_kernel,
        grid=(users // group,),
        in_specs=[pl.BlockSpec((group, slots), lambda i: (i, 0))] * 2,
        out_specs=pl.BlockSpec((n_blocks, group, height), lambda i: (0, i, 0)),
        out_shape=jax.ShapeDtypeStruct((n_blocks, users, height), F32),
        compiler_params=pltpu.CompilerParams(vmem_limit_bytes=32 * MIB),
        name="make_weights",
    )(refs, values)


def gram_kernel(refs, table, values, out, wide, picked):
    rows = table.shape[0]
    slots = refs.shape[2]
    chunk, unroll = 128, 32

    @pl.when(pl.program_id(0) == 0)
    def _():
        def widen(i, carry):
            part = table[pl.ds(i * chunk, chunk), :].astype(F32)
            wide[pl.ds(i * 2 * chunk, chunk, stride=2), :] = part[:, :128]
            wide[pl.ds(i * 2 * chunk + 1, chunk, stride=2), :] = part[:, 128:]
            return carry

        lax.fori_loop(0, rows // chunk, widen, 0)

    def fetch(i, carry):
        base = i * unroll
        got = [wide[pl.ds(pl.multiple_of(refs[0, 0, base + j] * 2, 2), 2), :] for j in range(unroll)]
        for j in range(unroll):
            picked[pl.ds(pl.multiple_of((base + j) * 2, 2), 2), :] = got[j]
        return carry

    lax.fori_loop(0, slots // unroll, fetch, 0)
    low = picked[pl.ds(0, slots, stride=2), :].astype(BF16)
    high = picked[pl.ds(1, slots, stride=2), :].astype(BF16)
    mat = jnp.concatenate([low, high], axis=1)
    gram = dot_tn(mat, mat)
    linear = lax.dot_general(
        jnp.broadcast_to(values[0], (8, slots)), mat, (((1,), (0,)), ((), ())), preferred_element_type=F32
    )
    r, c = iota((128, 128), 0), iota((128, 128), 1)
    last = gram[128:, 128:]
    out[0, :128, :] = jnp.where(r >= c, gram[:128, :128], last)
    out[0, 128:256, :] = gram[:128, 128:]
    diag = jnp.sum(jnp.where(r == c, last, 0.0), axis=0, keepdims=True)
    row = iota((8, 128), 0)
    tail = jnp.where(row == 1, linear[:, :128], jnp.where(row == 2, linear[:, 128:], 0.0))
    out[0, 256:264, :] = jnp.where(row == 0, diag, tail)


def gram_terms(table, refs, values):
    users, slots = refs.shape
    rows, rank = table.shape
    return pl.pallas_call(
        gram_kernel,
        grid=(users,),
        in_specs=[
            pl.BlockSpec((1, 1, slots), lambda u: (u, 0, 0), memory_space=pltpu.SMEM),
            pl.BlockSpec((rows, rank), lambda u: (0, 0), pipeline_mode=pl.Buffered(1)),
            pl.BlockSpec((1, 1, slots), lambda u: (u, 0, 0)),
        ],
        out_specs=pl.BlockSpec((1, 264, 128), lambda u: (u, 0, 0)),
        out_shape=jax.ShapeDtypeStruct((users, 264, 128), F32),
        scratch_shapes=[pltpu.VMEM((2 * rows, 128), F32), pltpu.VMEM((2 * slots, 128), F32)],
        compiler_params=pltpu.CompilerParams(vmem_limit_bytes=48 * MIB),
        name="gram_terms",
    )(refs.reshape(users, 1, slots), table, values.reshape(users, 1, slots))


def solve_kernel(packed, noise_cols, prior, shift, out, mats, right, back, sums):
    users = packed.shape[0]
    rank = prior.shape[0]
    half = rank // 2
    step, outer = 8, 64

    r, c = iota((half, half), 0), iota((half, half), 1)
    for m in range(users):
        both = packed[m, :half, :]
        cross = packed[m, half:rank, :]
        turned = both.T
        diag = packed[m, rank : rank + 1, :]
        first = jnp.where(r >= c, both, turned)
        last = jnp.where(r < c, both, jnp.where(r == c, diag, turned))
        mats[m, :half, :half] = prior[:half, :half] + ALPHA * first
        mats[m, :half, half:] = prior[:half, half:] + ALPHA * cross
        mats[m, half:, half:] = prior[half:, half:] + ALPHA * last
        mats[m, half:, :half] = jnp.zeros((half, half), F32)
        right[m, 0:1, :half] = ALPHA * packed[m, rank + 1 : rank + 2, :] + shift[:, :half]
        right[m, 0:1, half:] = ALPHA * packed[m, rank + 2 : rank + 3, :] + shift[:, half:]

    sub = iota((1, step, 128), 1)
    lane = iota((1, step, 128), 2)
    wide_lane = iota((step, rank), 1)
    unit = jnp.where(lane == sub + step, 1.0, 0.0)

    for o in range(rank // outer):
        lo = o * outer

        def panel(i, carry, lo=lo):
            k0 = pl.multiple_of(lo + i * step, step)
            rows = mats[:, pl.ds(k0, step), :]
            turn = (rank - k0) % rank
            aux = jnp.stack([pltpu.roll(rows[m], turn, 1)[:, :128] for m in range(users)])
            aux = jnp.where(lane < step, aux, unit)
            for k in range(step):
                col = aux[:, :, k : k + 1]
                factor = jnp.where(sub[:, :, :1] > k, col / col[:, k : k + 1, :], 0.0)
                aux = aux - factor * aux[:, k : k + 1, :]
                rows = rows - factor * rows[:, k : k + 1, :]
            pivots = jnp.sum(jnp.where(lane == sub, aux, 0.0), axis=2, keepdims=True)
            scale = lax.rsqrt(pivots)
            rows = rows * scale
            inverse = jnp.where((lane >= step) & (lane < 2 * step), aux * scale, 0.0)
            mats[:, pl.ds(k0, step), :] = rows
            noise = noise_cols[pl.ds(k0, step), :]
            for m in range(users):
                spread = jnp.concatenate([inverse[m], jnp.zeros((step, rank - 128), F32)], axis=1)
                spread = pltpu.roll(spread, (k0 + rank - step) % rank, 1)
                back[m, pl.ds(k0, step), :] = spread
                given = right[m, 0:1, :]
                y = jnp.sum(spread * given, axis=1, keepdims=True)
                right[m, 0:1, :] = given - jnp.sum(y * rows[m], axis=0, keepdims=True)
                sums[m, pl.ds(k0, step), :] = jnp.broadcast_to(y + noise[:, m : m + 1], (step, 128))
                hi, rest = split(rows[m])
                later = wide_lane >= k0 + step
                left = jnp.concatenate([hi, hi, rest, rest], axis=0)
                left = jnp.where(jnp.concatenate([later] * 4, axis=0), left, 0.0)[:, lo : lo + outer].astype(BF16)
                other = jnp.concatenate([hi, rest, hi, rest], axis=0).astype(BF16)
                mats[m, lo : lo + outer, :] = mats[m, lo : lo + outer, :] - dot_tn(left, other)
            return carry

        lax.fori_loop(0, outer // step, panel, 0)
        if lo + outer < rank:
            start = (lo + outer) // 128 * 128

            def trail(m, carry, lo=lo, start=start):
                left, other = stacked(mats[m, lo : lo + outer, :])
                mats[m, lo + outer :, start:] = mats[m, lo + outer :, start:] - dot_tn(
                    left[:, lo + outer :], other[:, start:]
                )
                return carry

            lax.fori_loop(0, users, trail, 0)

    def backward(i, x):
        k0 = pl.multiple_of(rank - step - i * step, step)
        rows = mats[:, pl.ds(k0, step), :]
        rest = sums[:, pl.ds(k0, step), :][:, :, :1] - jnp.sum(rows * x, axis=2, keepdims=True)
        return x + jnp.sum(back[:, pl.ds(k0, step), :] * rest, axis=1, keepdims=True)

    x = lax.fori_loop(0, rank // step, backward, jnp.zeros((users, 1, rank), F32))
    for m in range(users):
        out[m : m + 1, :] = x[m]


def solve_users(packed, noise, prior, shift):
    users = packed.shape[0]
    rank = prior.shape[0]
    vmem = pl.BlockSpec(memory_space=pltpu.VMEM)
    return pl.pallas_call(
        solve_kernel,
        in_specs=[vmem] * 4,
        out_specs=vmem,
        out_shape=jax.ShapeDtypeStruct((users, rank), F32),
        scratch_shapes=[
            pltpu.VMEM((users, rank, rank), F32),
            pltpu.VMEM((users, 8, rank), F32),
            pltpu.VMEM((users, rank, rank), F32),
            pltpu.VMEM((users, rank, 128), F32),
        ],
        compiler_params=pltpu.CompilerParams(vmem_limit_bytes=48 * MIB),
        name="solve_users",
    )(packed, noise.T, prior, shift.reshape(1, rank))


def stats_kernel(cols, listed, live, weights, samples, out):
    out[...] = jnp.zeros_like(out)

    def device(d, carry):
        hi, lo = split(samples[d])
        other = jnp.concatenate([hi, lo, hi, lo], axis=0).astype(BF16)
        for c in range(cols):
            i = d * cols + c
            own = jnp.where(live[i] > 0, ALPHA * weights[i], 0.0)
            hi, lo = split(own)
            left = jnp.concatenate([hi, hi, lo, lo], axis=0).astype(BF16)
            b = listed[i]
            out[b] = out[b] + dot_tn(left, other)
        return carry

    lax.fori_loop(0, samples.shape[0], device, 0)


def make_stats(weights, samples, listed, live, owned):
    n, users, height = weights.shape
    peers, _, rank = samples.shape
    vmem = pl.BlockSpec(memory_space=pltpu.VMEM)
    smem = pl.BlockSpec(memory_space=pltpu.SMEM)
    return pl.pallas_call(
        functools.partial(stats_kernel, n // peers),
        in_specs=[smem, smem, vmem, vmem],
        out_specs=vmem,
        out_shape=jax.ShapeDtypeStruct((owned, height, rank), F32),
        compiler_params=pltpu.CompilerParams(vmem_limit_bytes=32 * MIB),
        name="make_stats",
    )(listed, live, weights, samples)


def on_device(item_factors, send_ids, send_count, rating_pointer, rating_value, noise, prior_prec, prior_shift):
    peers = lax.axis_size("usr")
    blocks = item_factors[0]
    owned, height, rank = blocks.shape
    cols = send_ids.shape[-1]
    n = peers * cols
    listed = send_ids[0, 0].reshape(n)
    live = (jnp.arange(cols, dtype=jnp.int32)[None, :] < send_count[0, 0][:, None]).astype(jnp.int32).reshape(n)
    refs, values = rating_pointer[0], rating_value[0]

    outgoing = pick_blocks(blocks, listed, live)
    incoming = lax.all_to_all(outgoing, "usr", split_axis=0, concat_axis=0, tiled=True)
    weights = make_weights(refs, values, n, height)
    gathered = lax.all_to_all(weights, "usr", split_axis=0, concat_axis=0, tiled=True)

    packed = gram_terms(incoming.reshape(n * height, rank), refs, values)
    packed = lax.psum_scatter(packed, "grp", scatter_dimension=0, tiled=True)
    share = packed.shape[0]
    draws = lax.dynamic_slice_in_dim(noise, lax.axis_index("grp") * share, share, 0)
    own = solve_users(packed, draws, prior_prec, prior_shift)
    everyone = lax.all_gather(own, ("usr", "grp"), axis=0, tiled=True).reshape(peers, refs.shape[0], rank)
    samples = lax.dynamic_index_in_dim(everyone, lax.axis_index("usr"), 0, keepdims=False)
    stats = make_stats(gathered, everyone, listed, live, owned)
    return (samples, stats[None])


def solution(mesh):
    placed = (
        P("grp", "usr", None, None),
        P("grp", "usr", None, None),
        P("grp", "usr", None),
        P("grp", "usr", None),
        P("grp", "usr", None),
        P("usr", None),
        P(),
        P(),
    )
    return jax.shard_map(
        on_device,
        mesh=mesh,
        in_specs=placed,
        out_specs=(P("usr", None), P("grp", "usr", None, None)),
        check_vma=False,
    )
```

```python
import functools

import jax
import jax.numpy as jnp
from jax import lax
from jax.experimental import pallas as pl
from jax.experimental.pallas import tpu as pltpu
from jax.sharding import PartitionSpec as P

ALPHA = 2.0
F32 = jnp.float32
BF16 = jnp.bfloat16
MIB = 2**20


def iota(shape, dim):
    return lax.broadcasted_iota(jnp.int32, shape, dim)


def split(x):
    hi = x.astype(BF16).astype(F32)
    return hi, x - hi


def stacked(x):
    hi, lo = split(x)
    left = jnp.concatenate([hi, hi, lo, lo], axis=0).astype(BF16)
    right = jnp.concatenate([hi, lo, hi, lo], axis=0).astype(BF16)
    return left, right


def dot_tn(a, b):
    return lax.dot_general(a, b, (((0,), (0,)), ((), ())), preferred_element_type=F32)


def pick_kernel(cols, per_step, listed, live, blocks, out):
    base = pl.program_id(0) * per_step

    def body(i, carry):
        keep = live[base + i] > 0
        block = blocks[listed[base + i]]
        out[i] = jnp.where(keep, block, jnp.zeros_like(block))
        return carry

    lax.fori_loop(0, per_step, body, 0)


def pick_blocks(blocks, listed, live):
    n = listed.shape[0]
    owned, height, rank = blocks.shape
    steps = 4
    per_step = n // steps
    return pl.pallas_call(
        functools.partial(pick_kernel, n, per_step),
        grid_spec=pltpu.PrefetchScalarGridSpec(
            num_scalar_prefetch=2,
            grid=(steps,),
            in_specs=[pl.BlockSpec((owned, height, rank), lambda s, *_: (0, 0, 0))],
            out_specs=pl.BlockSpec((per_step, height, rank), lambda s, *_: (s, 0, 0)),
        ),
        out_shape=jax.ShapeDtypeStruct((n, height, rank), BF16),
        compiler_params=pltpu.CompilerParams(vmem_limit_bytes=32 * MIB),
        name="pick_blocks",
    )(listed, live, blocks)


def weight_kernel(refs, values, out):
    n_blocks, users, height = out.shape
    slots = refs.shape[1]
    for u in range(users):
        ref = refs[u : u + 1, :]
        value = values[u : u + 1, :].astype(F32)
        block = ref // height
        row = ref % height
        hot_block = jnp.where(iota((n_blocks, slots), 0) == block, value, 0.0).astype(BF16)
        hot_row = jnp.where(iota((height, slots), 0) == row, 1.0, 0.0).astype(BF16)
        out[:, u, :] = lax.dot_general(hot_block, hot_row, (((1,), (1,)), ((), ())), preferred_element_type=F32)


def make_weights(refs, values, n_blocks, height):
    users, slots = refs.shape
    group = 8
    return pl.pallas_call(
        weight_kernel,
        grid=(users // group,),
        in_specs=[pl.BlockSpec((group, slots), lambda i: (i, 0))] * 2,
        out_specs=pl.BlockSpec((n_blocks, group, height), lambda i: (0, i, 0)),
        out_shape=jax.ShapeDtypeStruct((n_blocks, users, height), F32),
        compiler_params=pltpu.CompilerParams(vmem_limit_bytes=32 * MIB),
        name="make_weights",
    )(refs, values)


def gather_rows(wide, picked, refs, user):
    slots = picked.shape[0] // 2
    unroll = 16
    for base in range(0, slots, unroll):
        got = [wide[pl.ds(pl.multiple_of(refs[user * slots + base + j], 2), 2), :] for j in range(unroll)]
        for j in range(unroll):
            picked[2 * (base + j) : 2 * (base + j) + 2, :] = got[j]


def packed_terms(picked, value, store):
    slots = picked.shape[0] // 2
    low = picked[pl.ds(0, slots, stride=2), :].astype(BF16)
    high = picked[pl.ds(1, slots, stride=2), :].astype(BF16)
    mat = jnp.concatenate([low, high], axis=1)
    gram = dot_tn(mat, mat)
    linear = lax.dot_general(
        jnp.broadcast_to(value, (8, slots)), mat, (((1,), (0,)), ((), ())), preferred_element_type=F32
    )
    r, c = iota((128, 128), 0), iota((128, 128), 1)
    last = gram[128:, 128:]
    store(0, jnp.where(r >= c, gram[:128, :128], last))
    store(128, gram[:128, 128:])
    diag = jnp.sum(jnp.where(r == c, last, 0.0), axis=0, keepdims=True)
    row = iota((8, 128), 0)
    tail = jnp.where(row == 1, linear[:, :128], jnp.where(row == 2, linear[:, 128:], 0.0))
    store(256, jnp.where(row == 0, diag, tail))


def gram_kernel(refs, table, values, out, wide, even, odd):
    rows = table.shape[0]
    users = out.shape[0]
    chunk = 128

    def widen(i, carry):
        part = table[pl.ds(i * chunk, chunk), :].astype(F32)
        wide[pl.ds(i * 2 * chunk, chunk, stride=2), :] = part[:, :128]
        wide[pl.ds(i * 2 * chunk + 1, chunk, stride=2), :] = part[:, 128:]
        return carry

    lax.fori_loop(0, rows // chunk, widen, 0)

    def terms(picked, u):
        def store(at, part):
            out[u, at : at + part.shape[0], :] = part

        packed_terms(picked, values[pl.ds(u, 1), :].astype(BF16), store)

    gather_rows(wide, even, refs, 0)

    def pair(i, carry):
        gather_rows(wide, odd, refs, 2 * i + 1)
        terms(even, 2 * i)
        gather_rows(wide, even, refs, lax.min(2 * i + 2, users - 1))
        terms(odd, 2 * i + 1)
        return carry

    lax.fori_loop(0, users // 2, pair, 0)


def gram_terms(table, refs, values):
    users, slots = refs.shape
    rows, rank = table.shape
    vmem = pl.BlockSpec(memory_space=pltpu.VMEM)
    return pl.pallas_call(
        gram_kernel,
        in_specs=[pl.BlockSpec(memory_space=pltpu.SMEM), vmem, vmem],
        out_specs=vmem,
        out_shape=jax.ShapeDtypeStruct((users, 264, 128), F32),
        scratch_shapes=[pltpu.VMEM((2 * rows, 128), F32)] + [pltpu.VMEM((2 * slots, 128), F32)] * 2,
        compiler_params=pltpu.CompilerParams(vmem_limit_bytes=48 * MIB),
        name="gram_terms",
    )((2 * refs).reshape(users * slots), table, values.astype(F32))


def solve_kernel(packed, noise_cols, prior, shift, out, mats, right, back, sums):
    users = packed.shape[0]
    rank = prior.shape[0]
    half = rank // 2
    step, outer = 8, 64

    r, c = iota((half, half), 0), iota((half, half), 1)
    for m in range(users):
        both = packed[m, :half, :]
        cross = packed[m, half:rank, :]
        turned = both.T
        diag = packed[m, rank : rank + 1, :]
        first = jnp.where(r >= c, both, turned)
        last = jnp.where(r < c, both, jnp.where(r == c, diag, turned))
        mats[m, :half, :half] = prior[:half, :half] + ALPHA * first
        mats[m, :half, half:] = prior[:half, half:] + ALPHA * cross
        mats[m, half:, half:] = prior[half:, half:] + ALPHA * last
        mats[m, half:, :half] = jnp.zeros((half, half), F32)
        right[m, 0:1, :half] = ALPHA * packed[m, rank + 1 : rank + 2, :] + shift[:, :half]
        right[m, 0:1, half:] = ALPHA * packed[m, rank + 2 : rank + 3, :] + shift[:, half:]

    sub = iota((1, step, 128), 1)
    lane = iota((1, step, 128), 2)
    wide_lane = iota((step, rank), 1)
    unit = jnp.where(lane == sub + step, 1.0, 0.0)

    for o in range(rank // outer):
        lo = o * outer

        def panel(i, carry, lo=lo):
            k0 = pl.multiple_of(lo + i * step, step)
            rows = mats[:, pl.ds(k0, step), :]
            turn = (rank - k0) % rank
            aux = jnp.stack([pltpu.roll(rows[m], turn, 1)[:, :128] for m in range(users)])
            aux = jnp.where(lane < step, aux, unit)
            for k in range(step):
                col = aux[:, :, k : k + 1]
                factor = jnp.where(sub[:, :, :1] > k, col / col[:, k : k + 1, :], 0.0)
                aux = aux - factor * aux[:, k : k + 1, :]
                rows = rows - factor * rows[:, k : k + 1, :]
            pivots = jnp.sum(jnp.where(lane == sub, aux, 0.0), axis=2, keepdims=True)
            scale = lax.rsqrt(pivots)
            rows = rows * scale
            inverse = jnp.where((lane >= step) & (lane < 2 * step), aux * scale, 0.0)
            mats[:, pl.ds(k0, step), :] = rows
            noise = noise_cols[pl.ds(k0, step), :]
            for m in range(users):
                spread = jnp.concatenate([inverse[m], jnp.zeros((step, rank - 128), F32)], axis=1)
                spread = pltpu.roll(spread, (k0 + rank - step) % rank, 1)
                back[m, pl.ds(k0, step), :] = spread
                given = right[m, 0:1, :]
                y = jnp.sum(spread * given, axis=1, keepdims=True)
                right[m, 0:1, :] = given - jnp.sum(y * rows[m], axis=0, keepdims=True)
                sums[m, pl.ds(k0, step), :] = jnp.broadcast_to(y + noise[:, m : m + 1], (step, 128))
                hi, rest = split(rows[m])
                later = wide_lane >= k0 + step
                left = jnp.concatenate([hi, hi, rest, rest], axis=0)
                left = jnp.where(jnp.concatenate([later] * 4, axis=0), left, 0.0)[:, lo : lo + outer].astype(BF16)
                other = jnp.concatenate([hi, rest, hi, rest], axis=0).astype(BF16)
                mats[m, lo : lo + outer, :] = mats[m, lo : lo + outer, :] - dot_tn(left, other)
            return carry

        lax.fori_loop(0, outer // step, panel, 0)
        if lo + outer < rank:
            start = (lo + outer) // 128 * 128

            def trail(m, carry, lo=lo, start=start):
                left, other = stacked(mats[m, lo : lo + outer, :])
                mats[m, lo + outer :, start:] = mats[m, lo + outer :, start:] - dot_tn(
                    left[:, lo + outer :], other[:, start:]
                )
                return carry

            lax.fori_loop(0, users, trail, 0)

    def backward(i, x):
        k0 = pl.multiple_of(rank - step - i * step, step)
        rows = mats[:, pl.ds(k0, step), :]
        rest = sums[:, pl.ds(k0, step), :][:, :, :1] - jnp.sum(rows * x, axis=2, keepdims=True)
        return x + jnp.sum(back[:, pl.ds(k0, step), :] * rest, axis=1, keepdims=True)

    x = lax.fori_loop(0, rank // step, backward, jnp.zeros((users, 1, rank), F32))
    for m in range(users):
        out[m : m + 1, :] = x[m]


def solve_users(packed, noise, prior, shift):
    users = packed.shape[0]
    rank = prior.shape[0]
    vmem = pl.BlockSpec(memory_space=pltpu.VMEM)
    return pl.pallas_call(
        solve_kernel,
        in_specs=[vmem] * 4,
        out_specs=vmem,
        out_shape=jax.ShapeDtypeStruct((users, rank), F32),
        scratch_shapes=[
            pltpu.VMEM((users, rank, rank), F32),
            pltpu.VMEM((users, 8, rank), F32),
            pltpu.VMEM((users, rank, rank), F32),
            pltpu.VMEM((users, rank, 128), F32),
        ],
        compiler_params=pltpu.CompilerParams(vmem_limit_bytes=48 * MIB),
        name="solve_users",
    )(packed, noise.T, prior, shift.reshape(1, rank))


def stats_kernel(cols, listed, live, weights, samples, out):
    out[...] = jnp.zeros_like(out)

    def device(d, carry):
        hi, lo = split(samples[d])
        other = jnp.concatenate([hi, lo, hi, lo], axis=0).astype(BF16)
        for c in range(cols):
            i = d * cols + c
            own = jnp.where(live[i] > 0, ALPHA * weights[i], 0.0)
            hi, lo = split(own)
            left = jnp.concatenate([hi, hi, lo, lo], axis=0).astype(BF16)
            b = listed[i]
            out[b] = out[b] + dot_tn(left, other)
        return carry

    lax.fori_loop(0, samples.shape[0], device, 0)


def make_stats(weights, samples, listed, live, owned):
    n, users, height = weights.shape
    peers, _, rank = samples.shape
    vmem = pl.BlockSpec(memory_space=pltpu.VMEM)
    smem = pl.BlockSpec(memory_space=pltpu.SMEM)
    return pl.pallas_call(
        functools.partial(stats_kernel, n // peers),
        in_specs=[smem, smem, vmem, vmem],
        out_specs=vmem,
        out_shape=jax.ShapeDtypeStruct((owned, height, rank), F32),
        compiler_params=pltpu.CompilerParams(vmem_limit_bytes=32 * MIB),
        name="make_stats",
    )(listed, live, weights, samples)


def on_device(item_factors, send_ids, send_count, rating_pointer, rating_value, noise, prior_prec, prior_shift):
    peers = lax.axis_size("usr")
    blocks = item_factors[0]
    owned, height, rank = blocks.shape
    cols = send_ids.shape[-1]
    n = peers * cols
    listed = send_ids[0, 0].reshape(n)
    live = (jnp.arange(cols, dtype=jnp.int32)[None, :] < send_count[0, 0][:, None]).astype(jnp.int32).reshape(n)
    refs, values = rating_pointer[0], rating_value[0]

    outgoing = pick_blocks(blocks, listed, live)
    incoming = lax.all_to_all(outgoing, "usr", split_axis=0, concat_axis=0, tiled=True)
    weights = make_weights(refs, values, n, height)
    incoming, weights = lax.optimization_barrier((incoming, weights))
    gathered = lax.all_to_all(weights, "usr", split_axis=0, concat_axis=0, tiled=True)

    packed = gram_terms(incoming.reshape(n * height, rank), refs, values)
    packed = lax.psum_scatter(packed, "grp", scatter_dimension=0, tiled=True)
    packed, gathered = lax.optimization_barrier((packed, gathered))
    share = packed.shape[0]
    draws = lax.dynamic_slice_in_dim(noise, lax.axis_index("grp") * share, share, 0)
    own = solve_users(packed, draws, prior_prec, prior_shift)
    everyone = lax.all_gather(own, ("usr", "grp"), axis=0, tiled=True).reshape(peers, refs.shape[0], rank)
    samples = lax.dynamic_index_in_dim(everyone, lax.axis_index("usr"), 0, keepdims=False)
    stats = make_stats(gathered, everyone, listed, live, owned)
    return (samples, stats[None])


def solution(mesh):
    placed = (
        P("grp", "usr", None, None),
        P("grp", "usr", None, None),
        P("grp", "usr", None),
        P("grp", "usr", None),
        P("grp", "usr", None),
        P("usr", None),
        P(),
        P(),
    )
    return jax.shard_map(
        on_device,
        mesh=mesh,
        in_specs=placed,
        out_specs=(P("usr", None), P("grp", "usr", None, None)),
        check_vma=False,
    )
```

```python
import functools

import jax
import jax.numpy as jnp
from jax import lax
from jax.experimental import pallas as pl
from jax.experimental.pallas import tpu as pltpu
from jax.sharding import PartitionSpec as P

ALPHA = 2.0
F32 = jnp.float32
BF16 = jnp.bfloat16
MIB = 2**20
MESH = pl.DeviceIdType.MESH


def iota(shape, dim):
    return lax.broadcasted_iota(jnp.int32, shape, dim)


def split(x):
    hi = x.astype(BF16).astype(F32)
    return hi, x - hi


def stacked(x):
    hi, lo = split(x)
    left = jnp.concatenate([hi, hi, lo, lo], axis=0).astype(BF16)
    right = jnp.concatenate([hi, lo, hi, lo], axis=0).astype(BF16)
    return left, right


def dot_tn(a, b):
    return lax.dot_general(a, b, (((0,), (0,)), ((), ())), preferred_element_type=F32)


def pick_kernel(cols, per_step, listed, live, blocks, out):
    base = pl.program_id(0) * per_step

    def body(i, carry):
        keep = live[base + i] > 0
        block = blocks[listed[base + i]]
        out[i] = jnp.where(keep, block, jnp.zeros_like(block))
        return carry

    lax.fori_loop(0, per_step, body, 0)


def pick_blocks(blocks, listed, live):
    n = listed.shape[0]
    owned, height, rank = blocks.shape
    steps = 4
    per_step = n // steps
    return pl.pallas_call(
        functools.partial(pick_kernel, n, per_step),
        grid_spec=pltpu.PrefetchScalarGridSpec(
            num_scalar_prefetch=2,
            grid=(steps,),
            in_specs=[pl.BlockSpec((owned, height, rank), lambda s, *_: (0, 0, 0))],
            out_specs=pl.BlockSpec((per_step, height, rank), lambda s, *_: (s, 0, 0)),
        ),
        out_shape=jax.ShapeDtypeStruct((n, height, rank), BF16),
        compiler_params=pltpu.CompilerParams(vmem_limit_bytes=32 * MIB),
        name="pick_blocks",
    )(listed, live, blocks)


def weight_kernel(refs, values, out):
    n_blocks, users, height = out.shape
    slots = refs.shape[1]
    for u in range(users):
        ref = refs[u : u + 1, :]
        value = values[u : u + 1, :].astype(F32)
        block = ref // height
        row = ref % height
        hot_block = jnp.where(iota((n_blocks, slots), 0) == block, value, 0.0).astype(BF16)
        hot_row = jnp.where(iota((height, slots), 0) == row, 1.0, 0.0).astype(BF16)
        out[:, u, :] = lax.dot_general(hot_block, hot_row, (((1,), (1,)), ((), ())), preferred_element_type=F32)


def make_weights(refs, values, n_blocks, height):
    users, slots = refs.shape
    group = 8
    return pl.pallas_call(
        weight_kernel,
        grid=(users // group,),
        in_specs=[pl.BlockSpec((group, slots), lambda i: (i, 0))] * 2,
        out_specs=pl.BlockSpec((n_blocks, group, height), lambda i: (0, i, 0)),
        out_shape=jax.ShapeDtypeStruct((n_blocks, users, height), F32),
        compiler_params=pltpu.CompilerParams(vmem_limit_bytes=32 * MIB),
        name="make_weights",
    )(refs, values)


def gather_rows(wide, picked, refs, user):
    slots = picked.shape[0] // 2
    unroll = 16
    for base in range(0, slots, unroll):
        got = [wide[pl.ds(refs[user * slots + base + j], 2), :] for j in range(unroll)]
        for j in range(unroll):
            picked[2 * (base + j) : 2 * (base + j) + 2, :] = got[j]


def packed_terms(picked, value, store):
    slots = picked.shape[0] // 2
    low = picked[pl.ds(0, slots, stride=2), :].astype(BF16)
    high = picked[pl.ds(1, slots, stride=2), :].astype(BF16)
    mat = jnp.concatenate([low, high], axis=1)
    gram = dot_tn(mat, mat)
    linear = lax.dot_general(
        jnp.broadcast_to(value, (8, slots)), mat, (((1,), (0,)), ((), ())), preferred_element_type=F32
    )
    r, c = iota((128, 128), 0), iota((128, 128), 1)
    last = gram[128:, 128:]
    store(0, jnp.where(r >= c, gram[:128, :128], last))
    store(128, gram[:128, 128:])
    diag = jnp.sum(jnp.where(r == c, last, 0.0), axis=0, keepdims=True)
    row = iota((8, 128), 0)
    tail = jnp.where(row == 1, linear[:, :128], jnp.where(row == 2, linear[:, 128:], 0.0))
    store(256, jnp.where(row == 0, diag, tail))


def gram_kernel(refs, table, values, out, wide, even, odd, stage, near, far, send_sem, recv_sem):
    rows = table.shape[0]
    share, height, _ = out.shape
    chunk, cut = 128, near.shape[2] // 16 * 8
    me, ring = lax.axis_index("grp"), 4
    after, before = (me + 1) % ring, (me + ring - 1) % ring

    barrier = pltpu.get_barrier_semaphore()
    for peer in (after, before):
        pl.semaphore_signal(barrier, inc=1, device_id={"grp": peer}, device_id_type=MESH)

    def widen(i, carry):
        part = table[pl.ds(i * chunk, chunk), :].astype(F32)
        wide[pl.ds(i * 2 * chunk, chunk, stride=2), :] = part[:, :128]
        wide[pl.ds(i * 2 * chunk + 1, chunk, stride=2), :] = part[:, 128:]
        return carry

    lax.fori_loop(0, rows // chunk, widen, 0)
    pl.semaphore_wait(barrier, 2)

    def copy(j, kind):
        if kind == 0:
            src, dst, peer = stage.at[2, j, :cut], far.at[0, j, :cut], after
        elif kind == 1:
            src, dst, peer = stage.at[2, j, cut:], far.at[1, j, cut:], before
        elif kind == 2:
            src, dst, peer = stage.at[1, j], near.at[0, j], after
        else:
            src, dst, peer = stage.at[3, j], near.at[1, j], before
        return pltpu.make_async_remote_copy(
            src_ref=src,
            dst_ref=dst,
            send_sem=send_sem.at[j, kind],
            recv_sem=recv_sem.at[j, kind],
            device_id={"grp": peer},
            device_id_type=MESH,
        )

    def user(j, kind):
        return (me + kind) % ring * share + j

    def terms(picked, j, kind):
        def store(at, part):
            stage[kind, j, at : at + part.shape[0], :] = part

        packed_terms(picked, values[pl.ds(user(j, kind), 1), :].astype(BF16), store)

    def pass_on(j):
        copy(j, 0).wait_recv()
        stage[1, j, :cut, :] = stage[1, j, :cut, :] + far[0, j, :cut, :]
        copy(j, 2).start()
        copy(j, 1).wait_recv()
        stage[3, j, cut:, :] = stage[3, j, cut:, :] + far[1, j, cut:, :]
        copy(j, 3).start()

    def finish(j):
        copy(j, 2).wait_recv()
        copy(j, 3).wait_recv()
        out[j] = stage[0, j] + near[0, j] + near[1, j]

    gather_rows(wide, even, refs, user(0, 2))

    def turn(j, carry):
        gather_rows(wide, odd, refs, user(j, 1))
        terms(even, j, 2)
        copy(j, 0).start()
        copy(j, 1).start()
        gather_rows(wide, even, refs, user(j, 3))
        terms(odd, j, 1)
        gather_rows(wide, odd, refs, user(j, 0))
        terms(even, j, 3)
        gather_rows(wide, even, refs, user((j + 1) % share, 2))
        terms(odd, j, 0)

        @pl.when(j >= 1)
        def _():
            pass_on(j - 1)

        @pl.when(j >= 2)
        def _():
            finish(j - 2)

        return carry

    lax.fori_loop(0, share, turn, 0)
    pass_on(share - 1)
    finish(share - 2)
    finish(share - 1)

    def drain(j, carry):
        for kind in range(4):
            copy(j, kind).wait_send()
        return carry

    lax.fori_loop(0, share, drain, 0)


def gram_terms(table, refs, values):
    users, slots = refs.shape
    rows, rank = table.shape
    ring, height = 4, 264
    share = users // ring
    vmem = pl.BlockSpec(memory_space=pltpu.VMEM)
    return pl.pallas_call(
        gram_kernel,
        in_specs=[pl.BlockSpec(memory_space=pltpu.SMEM), vmem, vmem],
        out_specs=vmem,
        out_shape=jax.ShapeDtypeStruct((share, height, 128), F32),
        scratch_shapes=[
            pltpu.VMEM((2 * rows, 128), F32),
            pltpu.VMEM((2 * slots, 128), F32),
            pltpu.VMEM((2 * slots, 128), F32),
            pltpu.VMEM((ring, share, height, 128), F32),
            pltpu.VMEM((2, share, height, 128), F32),
            pltpu.VMEM((2, share, height, 128), F32),
            pltpu.SemaphoreType.DMA((share, 4)),
            pltpu.SemaphoreType.DMA((share, 4)),
        ],
        compiler_params=pltpu.CompilerParams(vmem_limit_bytes=56 * MIB, collective_id=0, has_side_effects=True),
        cost_estimate=pl.CostEstimate(flops=60 * 10**9, bytes_accessed=200 * MIB, transcendentals=0),
        name="gram_terms",
    )((2 * refs).reshape(users * slots), table, values.astype(F32))


def solve_kernel(packed, noise_cols, prior, shift, out, mats, right, back, sums):
    users = packed.shape[0]
    rank = prior.shape[0]
    half = rank // 2
    step, outer = 8, 64

    r, c = iota((half, half), 0), iota((half, half), 1)
    for m in range(users):
        both = packed[m, :half, :]
        cross = packed[m, half:rank, :]
        turned = both.T
        diag = packed[m, rank : rank + 1, :]
        first = jnp.where(r >= c, both, turned)
        last = jnp.where(r < c, both, jnp.where(r == c, diag, turned))
        mats[m, :half, :half] = prior[:half, :half] + ALPHA * first
        mats[m, :half, half:] = prior[:half, half:] + ALPHA * cross
        mats[m, half:, half:] = prior[half:, half:] + ALPHA * last
        mats[m, half:, :half] = jnp.zeros((half, half), F32)
        right[m, 0:1, :half] = ALPHA * packed[m, rank + 1 : rank + 2, :] + shift[:, :half]
        right[m, 0:1, half:] = ALPHA * packed[m, rank + 2 : rank + 3, :] + shift[:, half:]

    sub = iota((1, step, 128), 1)
    lane = iota((1, step, 128), 2)
    wide_lane = iota((step, rank), 1)
    unit = jnp.where(lane == sub + step, 1.0, 0.0)

    for o in range(rank // outer):
        lo = o * outer

        def panel(i, carry, lo=lo):
            k0 = pl.multiple_of(lo + i * step, step)
            rows = mats[:, pl.ds(k0, step), :]
            turn = (rank - k0) % rank
            aux = jnp.stack([pltpu.roll(rows[m], turn, 1)[:, :128] for m in range(users)])
            aux = jnp.where(lane < step, aux, unit)
            for k in range(step):
                col = aux[:, :, k : k + 1]
                factor = jnp.where(sub[:, :, :1] > k, col / col[:, k : k + 1, :], 0.0)
                aux = aux - factor * aux[:, k : k + 1, :]
                rows = rows - factor * rows[:, k : k + 1, :]
            pivots = jnp.sum(jnp.where(lane == sub, aux, 0.0), axis=2, keepdims=True)
            scale = lax.rsqrt(pivots)
            rows = rows * scale
            inverse = jnp.where((lane >= step) & (lane < 2 * step), aux * scale, 0.0)
            mats[:, pl.ds(k0, step), :] = rows
            noise = noise_cols[pl.ds(k0, step), :]
            for m in range(users):
                spread = jnp.concatenate([inverse[m], jnp.zeros((step, rank - 128), F32)], axis=1)
                spread = pltpu.roll(spread, (k0 + rank - step) % rank, 1)
                back[m, pl.ds(k0, step), :] = spread
                given = right[m, 0:1, :]
                y = jnp.sum(spread * given, axis=1, keepdims=True)
                right[m, 0:1, :] = given - jnp.sum(y * rows[m], axis=0, keepdims=True)
                sums[m, pl.ds(k0, step), :] = jnp.broadcast_to(y + noise[:, m : m + 1], (step, 128))
                hi, rest = split(rows[m])
                later = wide_lane >= k0 + step
                left = jnp.concatenate([hi, hi, rest, rest], axis=0)
                left = jnp.where(jnp.concatenate([later] * 4, axis=0), left, 0.0)[:, lo : lo + outer].astype(BF16)
                other = jnp.concatenate([hi, rest, hi, rest], axis=0).astype(BF16)
                mats[m, lo : lo + outer, :] = mats[m, lo : lo + outer, :] - dot_tn(left, other)
            return carry

        lax.fori_loop(0, outer // step, panel, 0)
        if lo + outer < rank:
            start = (lo + outer) // 128 * 128

            def trail(m, carry, lo=lo, start=start):
                left, other = stacked(mats[m, lo : lo + outer, :])
                mats[m, lo + outer :, start:] = mats[m, lo + outer :, start:] - dot_tn(
                    left[:, lo + outer :], other[:, start:]
                )
                return carry

            lax.fori_loop(0, users, trail, 0)

    def backward(i, x):
        k0 = pl.multiple_of(rank - step - i * step, step)
        rows = mats[:, pl.ds(k0, step), :]
        rest = sums[:, pl.ds(k0, step), :][:, :, :1] - jnp.sum(rows * x, axis=2, keepdims=True)
        return x + jnp.sum(back[:, pl.ds(k0, step), :] * rest, axis=1, keepdims=True)

    x = lax.fori_loop(0, rank // step, backward, jnp.zeros((users, 1, rank), F32))
    for m in range(users):
        out[m : m + 1, :] = x[m]


def solve_users(packed, noise, prior, shift):
    users = packed.shape[0]
    rank = prior.shape[0]
    vmem = pl.BlockSpec(memory_space=pltpu.VMEM)
    return pl.pallas_call(
        solve_kernel,
        in_specs=[vmem] * 4,
        out_specs=vmem,
        out_shape=jax.ShapeDtypeStruct((users, rank), F32),
        scratch_shapes=[
            pltpu.VMEM((users, rank, rank), F32),
            pltpu.VMEM((users, 8, rank), F32),
            pltpu.VMEM((users, rank, rank), F32),
            pltpu.VMEM((users, rank, 128), F32),
        ],
        compiler_params=pltpu.CompilerParams(vmem_limit_bytes=48 * MIB),
        name="solve_users",
    )(packed, noise.T, prior, shift.reshape(1, rank))


def share_kernel(own, out, first_send, first_recv, send_sem, recv_sem, twin_send, twin_recv):
    g, u = lax.axis_index("grp"), lax.axis_index("usr")
    ring, side = 4, 4
    core, x, z = u % 2, u // 2 % side, u // (2 * side)
    twin = u + 1 - 2 * core
    moves = [(a, b) for a in range(side) for b in range(side) if a or b]

    def place(dz, dx):
        return (z + dz) % side * (2 * side) + (x + dx) % side * 2 + core

    barrier = pltpu.get_barrier_semaphore()
    for o in range(1, ring):
        pl.semaphore_signal(barrier, inc=1, device_id={"grp": (g + o) % ring}, device_id_type=MESH)
    for move in moves:
        pl.semaphore_signal(barrier, inc=1, device_id={"usr": place(*move)}, device_id_type=MESH)
    pl.semaphore_signal(barrier, inc=1, device_id={"usr": twin}, device_id_type=MESH)
    pl.semaphore_wait(barrier, ring + len(moves))

    def remote(src, dst, send, recv, peer):
        return pltpu.make_async_remote_copy(
            src_ref=src, dst_ref=dst, send_sem=send, recv_sem=recv, device_id=peer, device_id_type=MESH
        )

    first = [
        remote(own, out.at[u, g], first_send.at[o - 1], first_recv.at[o - 1], {"grp": (g + o) % ring})
        for o in range(1, ring)
    ]
    for c in first:
        c.start()
    out[u, g] = own[...]
    for o in range(1, ring):
        src = (g + ring - o) % ring
        remote(own, out.at[u, src], first_send.at[o - 1], first_recv.at[o - 1], {"grp": src}).wait_recv()
    slab = out.at[u]
    second = [
        remote(slab, slab, send_sem.at[k], recv_sem.at[k], {"usr": place(*move)}) for k, move in enumerate(moves)
    ]
    for c in second:
        c.start()
    to_twin = [remote(slab, slab, twin_send.at[len(moves)], twin_recv.at[len(moves)], {"usr": twin})]
    to_twin[0].start()
    for k, (dz, dx) in enumerate(moves):
        src = out.at[place(-dz + side, -dx + side)]
        remote(src, src, send_sem.at[k], recv_sem.at[k], {"usr": twin}).wait_recv()
        c = remote(src, src, twin_send.at[k], twin_recv.at[k], {"usr": twin})
        c.start()
        to_twin.append(c)
    for c in to_twin:
        c.wait_recv()
    for c in first + second + to_twin:
        c.wait_send()


def share_samples(own):
    share, rank = own.shape
    peers, ring = lax.axis_size("usr"), lax.axis_size("grp")
    vmem = pl.BlockSpec(memory_space=pltpu.VMEM)
    dma = pltpu.SemaphoreType.DMA
    return pl.pallas_call(
        share_kernel,
        in_specs=[vmem],
        out_specs=vmem,
        out_shape=jax.ShapeDtypeStruct((peers, ring, share, rank), F32),
        scratch_shapes=[dma((ring - 1,)), dma((ring - 1,)), dma((15,)), dma((15,)), dma((16,)), dma((16,))],
        compiler_params=pltpu.CompilerParams(vmem_limit_bytes=32 * MIB, collective_id=1, has_side_effects=True),
        name="share_samples",
    )(own)


def stats_kernel(cols, listed, live, weights, samples, out, held):
    out[...] = jnp.zeros_like(out)
    parts, share = samples.shape[1:3]

    def device(d, carry):
        for g in range(parts):
            held[g * share : (g + 1) * share, :] = samples[d, g]
        hi, lo = split(held[...])
        other = jnp.concatenate([hi, lo, hi, lo], axis=0).astype(BF16)
        for c in range(cols):
            i = d * cols + c
            own = jnp.where(live[i] > 0, ALPHA * weights[i], 0.0)
            hi, lo = split(own)
            left = jnp.concatenate([hi, hi, lo, lo], axis=0).astype(BF16)
            b = listed[i]
            out[b] = out[b] + dot_tn(left, other)
        return carry

    lax.fori_loop(0, samples.shape[0], device, 0)


def make_stats(weights, samples, listed, live, owned):
    n, users, height = weights.shape
    peers, _, _, rank = samples.shape
    vmem = pl.BlockSpec(memory_space=pltpu.VMEM)
    smem = pl.BlockSpec(memory_space=pltpu.SMEM)
    return pl.pallas_call(
        functools.partial(stats_kernel, n // peers),
        in_specs=[smem, smem, vmem, vmem],
        out_specs=vmem,
        out_shape=jax.ShapeDtypeStruct((owned, height, rank), F32),
        scratch_shapes=[pltpu.VMEM((users, rank), F32)],
        compiler_params=pltpu.CompilerParams(vmem_limit_bytes=32 * MIB),
        name="make_stats",
    )(listed, live, weights, samples)


def on_device(item_factors, send_ids, send_count, rating_pointer, rating_value, noise, prior_prec, prior_shift):
    peers = lax.axis_size("usr")
    blocks = item_factors[0]
    owned, height, rank = blocks.shape
    cols = send_ids.shape[-1]
    n = peers * cols
    listed = send_ids[0, 0].reshape(n)
    live = (jnp.arange(cols, dtype=jnp.int32)[None, :] < send_count[0, 0][:, None]).astype(jnp.int32).reshape(n)
    refs, values = rating_pointer[0], rating_value[0]

    outgoing = pick_blocks(blocks, listed, live)
    incoming = lax.all_to_all(outgoing, "usr", split_axis=0, concat_axis=0, tiled=True)
    weights = make_weights(refs, values, n, height)
    incoming, weights = lax.optimization_barrier((incoming, weights))
    gathered = lax.all_to_all(weights, "usr", split_axis=0, concat_axis=0, tiled=True)

    packed = gram_terms(incoming.reshape(n * height, rank), refs, values)
    packed, gathered = lax.optimization_barrier((packed, gathered))
    share = packed.shape[0]
    draws = lax.dynamic_slice_in_dim(noise, lax.axis_index("grp") * share, share, 0)
    everyone = share_samples(solve_users(packed, draws, prior_prec, prior_shift))
    samples = lax.dynamic_index_in_dim(everyone, lax.axis_index("usr"), 0, keepdims=False)
    samples = samples.reshape(refs.shape[0], rank)
    stats = make_stats(gathered, everyone, listed, live, owned)
    return (samples, stats[None])


def solution(mesh):
    placed = (
        P("grp", "usr", None, None),
        P("grp", "usr", None, None),
        P("grp", "usr", None),
        P("grp", "usr", None),
        P("grp", "usr", None),
        P("usr", None),
        P(),
        P(),
    )
    return jax.shard_map(
        on_device,
        mesh=mesh,
        in_specs=placed,
        out_specs=(P("usr", None), P("grp", "usr", None, None)),
        check_vma=False,
    )
```

```python
import functools

import jax
import jax.numpy as jnp
from jax import lax
from jax.experimental import pallas as pl
from jax.experimental.pallas import tpu as pltpu
from jax.sharding import PartitionSpec as P

ALPHA = 2.0
F32 = jnp.float32
BF16 = jnp.bfloat16
MIB = 2**20
MESH = pl.DeviceIdType.MESH


def iota(shape, dim):
    return lax.broadcasted_iota(jnp.int32, shape, dim)


def split(x):
    hi = x.astype(BF16).astype(F32)
    return hi, x - hi


def split3(x):
    hi = x.astype(BF16).astype(F32)
    rest = x - hi
    mid = rest.astype(BF16).astype(F32)
    return hi, mid, rest - mid


def stacked3(x):
    hi, mid, low = split3(x)
    left = jnp.concatenate([hi, hi, mid, hi, low, mid], axis=0).astype(BF16)
    right = jnp.concatenate([hi, mid, hi, low, hi, mid], axis=0).astype(BF16)
    return left, right


def dot_tn(a, b):
    return lax.dot_general(a, b, (((0,), (0,)), ((), ())), preferred_element_type=F32)


def pick_kernel(cols, per_step, listed, live, blocks, out):
    base = pl.program_id(0) * per_step

    def body(i, carry):
        keep = live[base + i] > 0
        block = blocks[listed[base + i]]
        out[i] = jnp.where(keep, block, jnp.zeros_like(block))
        return carry

    lax.fori_loop(0, per_step, body, 0)


def pick_blocks(blocks, listed, live):
    n = listed.shape[0]
    owned, height, rank = blocks.shape
    steps = 4
    per_step = n // steps
    return pl.pallas_call(
        functools.partial(pick_kernel, n, per_step),
        grid_spec=pltpu.PrefetchScalarGridSpec(
            num_scalar_prefetch=2,
            grid=(steps,),
            in_specs=[pl.BlockSpec((owned, height, rank), lambda s, *_: (0, 0, 0))],
            out_specs=pl.BlockSpec((per_step, height, rank), lambda s, *_: (s, 0, 0)),
        ),
        out_shape=jax.ShapeDtypeStruct((n, height, rank), BF16),
        compiler_params=pltpu.CompilerParams(vmem_limit_bytes=32 * MIB),
        name="pick_blocks",
    )(listed, live, blocks)


def weight_kernel(refs, values, out):
    n_blocks, users, height = out.shape
    slots = refs.shape[1]
    for u in range(users):
        ref = refs[u : u + 1, :]
        value = values[u : u + 1, :].astype(F32)
        block = ref // height
        row = ref % height
        hot_block = jnp.where(iota((n_blocks, slots), 0) == block, value, 0.0).astype(BF16)
        hot_row = jnp.where(iota((height, slots), 0) == row, 1.0, 0.0).astype(BF16)
        out[:, u, :] = lax.dot_general(hot_block, hot_row, (((1,), (1,)), ((), ())), preferred_element_type=F32)


def make_weights(refs, values, n_blocks, height):
    users, slots = refs.shape
    group = 8
    return pl.pallas_call(
        weight_kernel,
        grid=(users // group,),
        in_specs=[pl.BlockSpec((group, slots), lambda i: (i, 0))] * 2,
        out_specs=pl.BlockSpec((n_blocks, group, height), lambda i: (0, i, 0)),
        out_shape=jax.ShapeDtypeStruct((n_blocks, users, height), F32),
        compiler_params=pltpu.CompilerParams(vmem_limit_bytes=32 * MIB),
        name="make_weights",
    )(refs, values)


def gather_rows(wide, picked, refs, user):
    slots = picked.shape[0] // 2
    unroll = 16
    for base in range(0, slots, unroll):
        got = [wide[pl.ds(refs[user * slots + base + j], 2), :] for j in range(unroll)]
        for j in range(unroll):
            picked[2 * (base + j) : 2 * (base + j) + 2, :] = got[j]


def packed_terms(picked, value, store):
    slots = picked.shape[0] // 2
    low = picked[pl.ds(0, slots, stride=2), :].astype(BF16)
    high = picked[pl.ds(1, slots, stride=2), :].astype(BF16)
    mat = jnp.concatenate([low, high], axis=1)
    gram = dot_tn(mat, mat)
    linear = lax.dot_general(
        jnp.broadcast_to(value, (8, slots)), mat, (((1,), (0,)), ((), ())), preferred_element_type=F32
    )
    r, c = iota((128, 128), 0), iota((128, 128), 1)
    last = gram[128:, 128:]
    store(0, jnp.where(r >= c, gram[:128, :128], last))
    store(128, gram[:128, 128:])
    diag = jnp.sum(jnp.where(r == c, last, 0.0), axis=0, keepdims=True)
    row = iota((8, 128), 0)
    tail = jnp.where(row == 1, linear[:, :128], jnp.where(row == 2, linear[:, 128:], 0.0))
    store(256, jnp.where(row == 0, diag, tail))


def gram_kernel(refs, table, values, out, wide, even, odd, stage, near, far, send_sem, recv_sem):
    rows = table.shape[0]
    share, height, _ = out.shape
    chunk, cut = 128, near.shape[2] // 16 * 8
    me, ring = lax.axis_index("grp"), 4
    after, before = (me + 1) % ring, (me + ring - 1) % ring

    barrier = pltpu.get_barrier_semaphore()
    for peer in (after, before):
        pl.semaphore_signal(barrier, inc=1, device_id={"grp": peer}, device_id_type=MESH)

    def widen(i, carry):
        part = table[pl.ds(i * chunk, chunk), :].astype(F32)
        wide[pl.ds(i * 2 * chunk, chunk, stride=2), :] = part[:, :128]
        wide[pl.ds(i * 2 * chunk + 1, chunk, stride=2), :] = part[:, 128:]
        return carry

    lax.fori_loop(0, rows // chunk, widen, 0)
    pl.semaphore_wait(barrier, 2)

    def copy(j, kind):
        if kind == 0:
            src, dst, peer = stage.at[2, j, :cut], far.at[0, j, :cut], after
        elif kind == 1:
            src, dst, peer = stage.at[2, j, cut:], far.at[1, j, cut:], before
        elif kind == 2:
            src, dst, peer = stage.at[1, j], near.at[0, j], after
        else:
            src, dst, peer = stage.at[3, j], near.at[1, j], before
        return pltpu.make_async_remote_copy(
            src_ref=src,
            dst_ref=dst,
            send_sem=send_sem.at[j, kind],
            recv_sem=recv_sem.at[j, kind],
            device_id={"grp": peer},
            device_id_type=MESH,
        )

    def user(j, kind):
        return (me + kind) % ring * share + j

    def terms(picked, j, kind):
        def store(at, part):
            stage[kind, j, at : at + part.shape[0], :] = part

        packed_terms(picked, values[pl.ds(user(j, kind), 1), :].astype(BF16), store)

    def pass_on(j):
        copy(j, 0).wait_recv()
        stage[1, j, :cut, :] = stage[1, j, :cut, :] + far[0, j, :cut, :]
        copy(j, 2).start()
        copy(j, 1).wait_recv()
        stage[3, j, cut:, :] = stage[3, j, cut:, :] + far[1, j, cut:, :]
        copy(j, 3).start()

    def finish(j):
        copy(j, 2).wait_recv()
        copy(j, 3).wait_recv()
        out[j] = stage[0, j] + near[0, j] + near[1, j]

    gather_rows(wide, even, refs, user(0, 2))

    def turn(j, carry):
        gather_rows(wide, odd, refs, user(j, 1))
        terms(even, j, 2)
        copy(j, 0).start()
        copy(j, 1).start()
        gather_rows(wide, even, refs, user(j, 3))
        terms(odd, j, 1)
        gather_rows(wide, odd, refs, user(j, 0))
        terms(even, j, 3)
        gather_rows(wide, even, refs, user((j + 1) % share, 2))
        terms(odd, j, 0)

        @pl.when(j >= 1)
        def _():
            pass_on(j - 1)

        @pl.when(j >= 2)
        def _():
            finish(j - 2)

        return carry

    lax.fori_loop(0, share, turn, 0)
    pass_on(share - 1)
    finish(share - 2)
    finish(share - 1)

    def drain(j, carry):
        for kind in range(4):
            copy(j, kind).wait_send()
        return carry

    lax.fori_loop(0, share, drain, 0)


def gram_terms(table, refs, values):
    users, slots = refs.shape
    rows, rank = table.shape
    ring, height = 4, 264
    share = users // ring
    vmem = pl.BlockSpec(memory_space=pltpu.VMEM)
    return pl.pallas_call(
        gram_kernel,
        in_specs=[pl.BlockSpec(memory_space=pltpu.SMEM), vmem, vmem],
        out_specs=vmem,
        out_shape=jax.ShapeDtypeStruct((share, height, 128), F32),
        scratch_shapes=[
            pltpu.VMEM((2 * rows, 128), F32),
            pltpu.VMEM((2 * slots, 128), F32),
            pltpu.VMEM((2 * slots, 128), F32),
            pltpu.VMEM((ring, share, height, 128), F32),
            pltpu.VMEM((2, share, height, 128), F32),
            pltpu.VMEM((2, share, height, 128), F32),
            pltpu.SemaphoreType.DMA((share, 4)),
            pltpu.SemaphoreType.DMA((share, 4)),
        ],
        compiler_params=pltpu.CompilerParams(vmem_limit_bytes=56 * MIB, collective_id=0, has_side_effects=True),
        cost_estimate=pl.CostEstimate(flops=60 * 10**9, bytes_accessed=200 * MIB, transcendentals=0),
        name="gram_terms",
    )((2 * refs).reshape(users * slots), table, values.astype(F32))


def solve_kernel(packed, noise_cols, prior, shift, out, mats, right, back, sums):
    users = packed.shape[0]
    rank = prior.shape[0]
    half = rank // 2
    step = 32

    r, c = iota((half, half), 0), iota((half, half), 1)
    for m in range(users):
        both = packed[m, :half, :]
        cross = packed[m, half:rank, :]
        turned = both.T
        diag = packed[m, rank : rank + 1, :]
        first = jnp.where(r >= c, both, turned)
        last = jnp.where(r < c, both, jnp.where(r == c, diag, turned))
        mats[m, :half, :half] = prior[:half, :half] + ALPHA * first
        mats[m, :half, half:] = prior[:half, half:] + ALPHA * cross
        mats[m, half:, half:] = prior[half:, half:] + ALPHA * last
        right[m, 0:1, :half] = ALPHA * packed[m, rank + 1 : rank + 2, :] + shift[:, :half]
        right[m, 0:1, half:] = ALPHA * packed[m, rank + 2 : rank + 3, :] + shift[:, half:]

    sub = iota((1, 8, 128), 1)
    lane = iota((1, 8, 128), 2)
    tall_lane = iota((step, 128), 1)

    def column(x, k):
        return jnp.broadcast_to(x[:, :, k : k + 1], x.shape)

    for k0 in range(0, rank, step):
        tile, group = k0 // half * half, k0 % half // step
        parts, pivots = [], []
        for h in range(step // 8):
            rows = mats[:, k0 + 8 * h : k0 + 8 * h + 8, tile : tile + half]
            if group:
                rows = jnp.stack([pltpu.roll(rows[m], half - group * step, 1) for m in range(users)])
            unit = jnp.where(lane % step == sub + 8 * h, 1.0, 0.0)
            parts.append(jnp.where(lane < step, rows, unit))
            pivots.append(jnp.ones((users, 8, 128), F32))
        for k in range(0, step, 2):
            f, kk = k // 8, k % 8
            ones = [column(parts[h], k) for h in range(f, step // 8)]
            twos = [column(parts[h], k + 1) for h in range(f, step // 8)]
            a, b, c = ones[0][:, kk : kk + 1, :], twos[0][:, kk : kk + 1, :], twos[0][:, kk + 1 : kk + 2, :]
            low, high = parts[f][:, kk : kk + 1, :], parts[f][:, kk + 1 : kk + 2, :]
            inv = 1.0 / (a * c - b * b)
            ratio = b * (1.0 / a)
            first = (c * low - b * high) * inv
            second = (a * high - b * low) * inv
            second_row = parts[f] - ratio * low
            pivots[f] = jnp.where(sub == kk, a, jnp.where(sub == kk + 1, c - ratio * b, pivots[f]))
            for h in range(f, step // 8):
                new = parts[h] - ones[h - f] * first - twos[h - f] * second
                if h == f:
                    new = jnp.where(sub > kk + 1, new, jnp.where(sub == kk + 1, second_row, parts[h]))
                parts[h] = new
        scaled = [p * lax.rsqrt(v) for p, v in zip(parts, pivots)]
        for m in range(users):
            turn = jnp.concatenate([x[m] for x in scaled], axis=0)
            hi, mid, low = split3(turn)
            one = jnp.where(tall_lane < step, 0.0, jnp.where(tall_lane < 3 * step, hi, mid))
            two = jnp.where(tall_lane < step, 0.0, jnp.where(tall_lane < 2 * step, hi, jnp.where(tall_lane < 3 * step, low, mid)))
            left = jnp.concatenate([one, two], axis=1).astype(BF16)
            hi, mid, low = split3(mats[m, k0 : k0 + step, tile:])
            other = jnp.concatenate([hi, hi, mid, hi, hi, low, hi, mid], axis=0).astype(BF16)
            rows = jnp.dot(left, other, preferred_element_type=F32)
            mats[m, k0 : k0 + step, tile:] = rows
            if not group:
                turn = pltpu.roll(turn, half - step, 1)
            keep = (tall_lane >= group * step) & (tall_lane < (group + 1) * step)
            turn = jnp.where(keep, turn, 0.0)
            back[m, k0 : k0 + step, :] = turn
            y = jnp.sum(turn * right[m, 0:1, tile : tile + half], axis=1, keepdims=True)
            right[m, 0:1, tile:] = right[m, 0:1, tile:] - jnp.sum(y * rows, axis=0, keepdims=True)
            sums[m, k0 : k0 + step, :] = jnp.broadcast_to(y + noise_cols[k0 : k0 + step, m : m + 1], (step, 128))
            low = k0 + step
            start = low // half * half
            if low < rank:
                left, other = stacked3(rows[:, start - tile :])
                change = dot_tn(left, other)
                mats[m, low:, start:] = mats[m, low:, start:] - change[low - start :]

    x = [jnp.zeros((users, 1, half), F32)] * 2
    for k0 in range(rank - step, -1, -step):
        t = k0 // half
        at = pl.ds(k0, step)
        part = mats[:, at, half:] * x[1]
        if t == 0:
            part = part + mats[:, at, :half] * x[0]
        rest = sums[:, at, :] - jnp.sum(part, axis=2, keepdims=True)
        x[t] = x[t] + jnp.sum(back[:, at, :] * rest, axis=1, keepdims=True)
    for m in range(users):
        out[m : m + 1, :half] = x[0][m]
        out[m : m + 1, half:] = x[1][m]


def solve_users(packed, noise, prior, shift):
    users = packed.shape[0]
    rank = prior.shape[0]
    vmem = pl.BlockSpec(memory_space=pltpu.VMEM)
    return pl.pallas_call(
        solve_kernel,
        in_specs=[vmem] * 4,
        out_specs=vmem,
        out_shape=jax.ShapeDtypeStruct((users, rank), F32),
        scratch_shapes=[
            pltpu.VMEM((users, rank, rank), F32),
            pltpu.VMEM((users, 8, rank), F32),
            pltpu.VMEM((users, rank, 128), F32),
            pltpu.VMEM((users, rank, 128), F32),
        ],
        compiler_params=pltpu.CompilerParams(vmem_limit_bytes=48 * MIB),
        name="solve_users",
    )(packed, noise.T, prior, shift.reshape(1, rank))


def share_kernel(own, out, first_send, first_recv, send_sem, recv_sem, twin_send, twin_recv):
    g, u = lax.axis_index("grp"), lax.axis_index("usr")
    ring, side = 4, 4
    core, x, z = u % 2, u // 2 % side, u // (2 * side)
    twin = u + 1 - 2 * core
    moves = [(a, b) for a in range(side) for b in range(side) if a or b]

    def place(dz, dx):
        return (z + dz) % side * (2 * side) + (x + dx) % side * 2 + core

    barrier = pltpu.get_barrier_semaphore()
    for o in range(1, ring):
        pl.semaphore_signal(barrier, inc=1, device_id={"grp": (g + o) % ring}, device_id_type=MESH)
    for move in moves:
        pl.semaphore_signal(barrier, inc=1, device_id={"usr": place(*move)}, device_id_type=MESH)
    pl.semaphore_signal(barrier, inc=1, device_id={"usr": twin}, device_id_type=MESH)
    pl.semaphore_wait(barrier, ring + len(moves))

    def remote(src, dst, send, recv, peer):
        return pltpu.make_async_remote_copy(
            src_ref=src, dst_ref=dst, send_sem=send, recv_sem=recv, device_id=peer, device_id_type=MESH
        )

    first = [
        remote(own, out.at[u, g], first_send.at[o - 1], first_recv.at[o - 1], {"grp": (g + o) % ring})
        for o in range(1, ring)
    ]
    for c in first:
        c.start()
    out[u, g] = own[...]
    for o in range(1, ring):
        src = (g + ring - o) % ring
        remote(own, out.at[u, src], first_send.at[o - 1], first_recv.at[o - 1], {"grp": src}).wait_recv()
    slab = out.at[u]
    second = [
        remote(slab, slab, send_sem.at[k], recv_sem.at[k], {"usr": place(*move)}) for k, move in enumerate(moves)
    ]
    for c in second:
        c.start()
    to_twin = [remote(slab, slab, twin_send.at[len(moves)], twin_recv.at[len(moves)], {"usr": twin})]
    to_twin[0].start()
    for k, (dz, dx) in enumerate(moves):
        src = out.at[place(-dz + side, -dx + side)]
        remote(src, src, send_sem.at[k], recv_sem.at[k], {"usr": twin}).wait_recv()
        c = remote(src, src, twin_send.at[k], twin_recv.at[k], {"usr": twin})
        c.start()
        to_twin.append(c)
    for c in to_twin:
        c.wait_recv()
    for c in first + second + to_twin:
        c.wait_send()


def share_samples(own):
    share, rank = own.shape
    peers, ring = lax.axis_size("usr"), lax.axis_size("grp")
    vmem = pl.BlockSpec(memory_space=pltpu.VMEM)
    dma = pltpu.SemaphoreType.DMA
    return pl.pallas_call(
        share_kernel,
        in_specs=[vmem],
        out_specs=vmem,
        out_shape=jax.ShapeDtypeStruct((peers, ring, share, rank), F32),
        scratch_shapes=[dma((ring - 1,)), dma((ring - 1,)), dma((15,)), dma((15,)), dma((16,)), dma((16,))],
        compiler_params=pltpu.CompilerParams(vmem_limit_bytes=32 * MIB, collective_id=1, has_side_effects=True),
        name="share_samples",
    )(own)


def stats_kernel(cols, listed, live, weights, samples, out, held):
    out[...] = jnp.zeros_like(out)
    parts, share = samples.shape[1:3]

    def device(d, carry):
        for g in range(parts):
            held[g * share : (g + 1) * share, :] = samples[d, g]
        hi, lo = split(held[...])
        other = jnp.concatenate([hi, lo, hi, lo], axis=0).astype(BF16)
        terms = []
        for c in range(cols):
            hi, lo = split(jnp.where(live[d * cols + c] > 0, ALPHA * weights[d * cols + c], 0.0))
            left = jnp.concatenate([hi, hi, lo, lo], axis=0).astype(BF16)
            terms.append(dot_tn(left, other))
        for c in range(cols):
            b = listed[d * cols + c]
            out[b] = out[b] + terms[c]
        return carry

    lax.fori_loop(0, samples.shape[0], device, 0)


def make_stats(weights, samples, listed, live, owned):
    n, users, height = weights.shape
    peers, _, _, rank = samples.shape
    vmem = pl.BlockSpec(memory_space=pltpu.VMEM)
    smem = pl.BlockSpec(memory_space=pltpu.SMEM)
    return pl.pallas_call(
        functools.partial(stats_kernel, n // peers),
        in_specs=[smem, smem, vmem, vmem],
        out_specs=vmem,
        out_shape=jax.ShapeDtypeStruct((owned, height, rank), F32),
        scratch_shapes=[pltpu.VMEM((users, rank), F32)],
        compiler_params=pltpu.CompilerParams(vmem_limit_bytes=32 * MIB),
        name="make_stats",
    )(listed, live, weights, samples)


def on_device(item_factors, send_ids, send_count, rating_pointer, rating_value, noise, prior_prec, prior_shift):
    peers = lax.axis_size("usr")
    blocks = item_factors[0]
    owned, height, rank = blocks.shape
    cols = send_ids.shape[-1]
    n = peers * cols
    listed = send_ids[0, 0].reshape(n)
    live = (jnp.arange(cols, dtype=jnp.int32)[None, :] < send_count[0, 0][:, None]).astype(jnp.int32).reshape(n)
    refs, values = rating_pointer[0], rating_value[0]

    outgoing = pick_blocks(blocks, listed, live)
    incoming = lax.all_to_all(outgoing, "usr", split_axis=0, concat_axis=0, tiled=True)
    weights = make_weights(refs, values, n, height)
    incoming, weights = lax.optimization_barrier((incoming, weights))
    gathered = lax.all_to_all(weights, "usr", split_axis=0, concat_axis=0, tiled=True)

    packed = gram_terms(incoming.reshape(n * height, rank), refs, values)
    packed, gathered = lax.optimization_barrier((packed, gathered))
    share = packed.shape[0]
    draws = lax.dynamic_slice_in_dim(noise, lax.axis_index("grp") * share, share, 0)
    everyone = share_samples(solve_users(packed, draws, prior_prec, prior_shift))
    samples = lax.dynamic_index_in_dim(everyone, lax.axis_index("usr"), 0, keepdims=False)
    samples = samples.reshape(refs.shape[0], rank)
    stats = make_stats(gathered, everyone, listed, live, owned)
    return (samples, stats[None])


def solution(mesh):
    placed = (
        P("grp", "usr", None, None),
        P("grp", "usr", None, None),
        P("grp", "usr", None),
        P("grp", "usr", None),
        P("grp", "usr", None),
        P("usr", None),
        P(),
        P(),
    )
    return jax.shard_map(
        on_device,
        mesh=mesh,
        in_specs=placed,
        out_specs=(P("usr", None), P("grp", "usr", None, None)),
        check_vma=False,
    )
```

```python
import functools

import jax
import jax.numpy as jnp
from jax import lax
from jax.experimental import pallas as pl
from jax.experimental.pallas import tpu as pltpu
from jax.sharding import PartitionSpec as P

ALPHA = 2.0
F32 = jnp.float32
BF16 = jnp.bfloat16
MIB = 2**20
MESH = pl.DeviceIdType.MESH


def iota(shape, dim):
    return lax.broadcasted_iota(jnp.int32, shape, dim)


def split(x):
    hi = x.astype(BF16).astype(F32)
    return hi, x - hi


def split3(x):
    hi = x.astype(BF16).astype(F32)
    rest = x - hi
    mid = rest.astype(BF16).astype(F32)
    return hi, mid, rest - mid


def stacked3(x):
    hi, mid, low = split3(x)
    left = jnp.concatenate([hi, hi, mid, hi, low, mid], axis=0).astype(BF16)
    right = jnp.concatenate([hi, mid, hi, low, hi, mid], axis=0).astype(BF16)
    return left, right


def dot_tn(a, b):
    return lax.dot_general(a, b, (((0,), (0,)), ((), ())), preferred_element_type=F32)


def pick_kernel(listed, live, blocks, out, zeros, sems):
    n = out.shape[0]
    zeros[...] = jnp.zeros_like(zeros)

    def start(i, carry):
        @pl.when(live[i] > 0)
        def _():
            pltpu.make_async_copy(blocks.at[listed[i]], out.at[i], sems.at[i]).start()

        @pl.when(live[i] <= 0)
        def _():
            pltpu.make_async_copy(zeros, out.at[i], sems.at[i]).start()

        return carry

    def wait(i, carry):
        pltpu.make_async_copy(zeros, out.at[i], sems.at[i]).wait()
        return carry

    lax.fori_loop(0, n, start, 0)
    lax.fori_loop(0, n, wait, 0)


def pick_blocks(blocks, listed, live):
    n = listed.shape[0]
    owned, height, rank = blocks.shape
    smem = pl.BlockSpec(memory_space=pltpu.SMEM)
    return pl.pallas_call(
        pick_kernel,
        in_specs=[smem, smem, pl.BlockSpec(memory_space=pltpu.HBM)],
        out_specs=pl.BlockSpec(memory_space=pltpu.HBM),
        out_shape=jax.ShapeDtypeStruct((n, height, rank), BF16),
        scratch_shapes=[pltpu.VMEM((height, rank), BF16), pltpu.SemaphoreType.DMA((n,))],
        compiler_params=pltpu.CompilerParams(vmem_limit_bytes=32 * MIB),
        name="pick_blocks",
    )(listed, live, blocks)


def weight_kernel(refs, values, out):
    n_blocks, users, height = out.shape
    slots = refs.shape[1]
    for u in range(users):
        ref = refs[u : u + 1, :]
        value = values[u : u + 1, :].astype(F32)
        block = ref // height
        row = ref % height
        hot_block = jnp.where(iota((n_blocks, slots), 0) == block, value, 0.0).astype(BF16)
        hot_row = jnp.where(iota((height, slots), 0) == row, 1.0, 0.0).astype(BF16)
        out[:, u, :] = lax.dot_general(hot_block, hot_row, (((1,), (1,)), ((), ())), preferred_element_type=F32)


def make_weights(refs, values, n_blocks, height):
    users, slots = refs.shape
    group = 8
    return pl.pallas_call(
        weight_kernel,
        grid=(users // group,),
        in_specs=[pl.BlockSpec((group, slots), lambda i: (i, 0))] * 2,
        out_specs=pl.BlockSpec((n_blocks, group, height), lambda i: (0, i, 0)),
        out_shape=jax.ShapeDtypeStruct((n_blocks, users, height), F32),
        compiler_params=pltpu.CompilerParams(vmem_limit_bytes=32 * MIB),
        name="make_weights",
    )(refs, values)


def gather_rows(wide, picked, refs, user):
    slots = picked.shape[0] // 2
    unroll = 16
    for base in range(0, slots, unroll):
        got = [wide[pl.ds(refs[user * slots + base + j], 2), :] for j in range(unroll)]
        for j in range(unroll):
            picked[2 * (base + j) : 2 * (base + j) + 2, :] = got[j]


def packed_terms(picked, value, store):
    slots = picked.shape[0] // 2
    low = picked[pl.ds(0, slots, stride=2), :].astype(BF16)
    high = picked[pl.ds(1, slots, stride=2), :].astype(BF16)
    mat = jnp.concatenate([low, high], axis=1)
    gram = dot_tn(mat, mat)
    linear = lax.dot_general(
        jnp.broadcast_to(value, (8, slots)), mat, (((1,), (0,)), ((), ())), preferred_element_type=F32
    )
    r, c = iota((128, 128), 0), iota((128, 128), 1)
    last = gram[128:, 128:]
    store(0, jnp.where(r >= c, gram[:128, :128], last))
    store(128, gram[:128, 128:])
    diag = jnp.sum(jnp.where(r == c, last, 0.0), axis=0, keepdims=True)
    row = iota((8, 128), 0)
    tail = jnp.where(row == 1, linear[:, :128], jnp.where(row == 2, linear[:, 128:], 0.0))
    store(256, jnp.where(row == 0, diag, tail))


def gram_kernel(
    refs, table, values, weights, out, gathered, wide, even, odd, stage, near, far, send_sem, recv_sem, give_sem, take_sem, own_sem
):
    rows = table.shape[0]
    share, height, _ = out.shape
    chunk, cut = 128, near.shape[2] // 16 * 8
    me, ring = lax.axis_index("grp"), 4
    after, before = (me + 1) % ring, (me + ring - 1) % ring
    u, peers = lax.axis_index("usr"), lax.axis_size("usr")
    cols = weights.shape[0] // peers

    barrier = pltpu.get_barrier_semaphore()
    for peer in (after, before):
        pl.semaphore_signal(barrier, inc=1, device_id={"grp": peer}, device_id_type=MESH)
    for o in range(1, peers):
        pl.semaphore_signal(barrier, inc=1, device_id={"usr": (u + o) % peers}, device_id_type=MESH)

    def give(o):
        peer = (u + o) % peers
        return pltpu.make_async_remote_copy(
            src_ref=weights.at[pl.ds(peer * cols, cols)],
            dst_ref=gathered.at[pl.ds(u * cols, cols)],
            send_sem=give_sem.at[o],
            recv_sem=take_sem.at[o],
            device_id={"usr": peer},
            device_id_type=MESH,
        )

    def take(o):
        peer = (u + peers - o) % peers
        slab = gathered.at[pl.ds(peer * cols, cols)]
        return pltpu.make_async_remote_copy(
            src_ref=slab,
            dst_ref=slab,
            send_sem=give_sem.at[o],
            recv_sem=take_sem.at[o],
            device_id={"usr": peer},
            device_id_type=MESH,
        )

    def widen(i, carry):
        part = table[pl.ds(i * chunk, chunk), :].astype(F32)
        wide[pl.ds(i * 2 * chunk, chunk, stride=2), :] = part[:, :128]
        wide[pl.ds(i * 2 * chunk + 1, chunk, stride=2), :] = part[:, 128:]
        return carry

    lax.fori_loop(0, rows // chunk, widen, 0)
    pl.semaphore_wait(barrier, peers + 1)

    keep = pltpu.make_async_copy(
        weights.at[pl.ds(u * cols, cols)], gathered.at[pl.ds(u * cols, cols)], own_sem
    )
    keep.start()

    def send_weights(o, carry):
        give(o).start()
        return carry

    lax.fori_loop(1, peers, send_weights, 0)

    def copy(j, kind):
        if kind == 0:
            src, dst, peer = stage.at[2, j, :cut], far.at[0, j, :cut], after
        elif kind == 1:
            src, dst, peer = stage.at[2, j, cut:], far.at[1, j, cut:], before
        elif kind == 2:
            src, dst, peer = stage.at[1, j], near.at[0, j], after
        else:
            src, dst, peer = stage.at[3, j], near.at[1, j], before
        return pltpu.make_async_remote_copy(
            src_ref=src,
            dst_ref=dst,
            send_sem=send_sem.at[j, kind],
            recv_sem=recv_sem.at[j, kind],
            device_id={"grp": peer},
            device_id_type=MESH,
        )

    def user(j, kind):
        return (me + kind) % ring * share + j

    def terms(picked, j, kind):
        def store(at, part):
            stage[kind, j, at : at + part.shape[0], :] = part

        packed_terms(picked, values[pl.ds(user(j, kind), 1), :].astype(BF16), store)

    def pass_on(j):
        copy(j, 0).wait_recv()
        stage[1, j, :cut, :] = stage[1, j, :cut, :] + far[0, j, :cut, :]
        copy(j, 2).start()
        copy(j, 1).wait_recv()
        stage[3, j, cut:, :] = stage[3, j, cut:, :] + far[1, j, cut:, :]
        copy(j, 3).start()

    def finish(j):
        copy(j, 2).wait_recv()
        copy(j, 3).wait_recv()
        out[j] = stage[0, j] + near[0, j] + near[1, j]

    gather_rows(wide, even, refs, user(0, 2))

    def turn(j, carry):
        gather_rows(wide, odd, refs, user(j, 1))
        terms(even, j, 2)
        copy(j, 0).start()
        copy(j, 1).start()
        gather_rows(wide, even, refs, user(j, 3))
        terms(odd, j, 1)
        gather_rows(wide, odd, refs, user(j, 0))
        terms(even, j, 3)
        gather_rows(wide, even, refs, user((j + 1) % share, 2))
        terms(odd, j, 0)

        @pl.when(j >= 1)
        def _():
            pass_on(j - 1)

        @pl.when(j >= 2)
        def _():
            finish(j - 2)

        return carry

    lax.fori_loop(0, share, turn, 0)
    pass_on(share - 1)
    finish(share - 2)
    finish(share - 1)

    def drain(j, carry):
        for kind in range(4):
            copy(j, kind).wait_send()
        return carry

    lax.fori_loop(0, share, drain, 0)

    def drain_weights(o, carry):
        give(o).wait_send()
        take(o).wait_recv()
        return carry

    lax.fori_loop(1, peers, drain_weights, 0)
    keep.wait()


def gram_terms(table, refs, values, weights):
    users, slots = refs.shape
    rows, rank = table.shape
    ring, height = 4, 264
    share = users // ring
    peers = lax.axis_size("usr")
    vmem = pl.BlockSpec(memory_space=pltpu.VMEM)
    hbm = pl.BlockSpec(memory_space=pltpu.HBM)
    return pl.pallas_call(
        gram_kernel,
        in_specs=[pl.BlockSpec(memory_space=pltpu.SMEM), vmem, vmem, hbm],
        out_specs=(vmem, hbm),
        out_shape=(
            jax.ShapeDtypeStruct((share, height, 128), F32),
            jax.ShapeDtypeStruct(weights.shape, F32),
        ),
        scratch_shapes=[
            pltpu.VMEM((2 * rows, 128), F32),
            pltpu.VMEM((2 * slots, 128), F32),
            pltpu.VMEM((2 * slots, 128), F32),
            pltpu.VMEM((ring, share, height, 128), F32),
            pltpu.VMEM((2, share, height, 128), F32),
            pltpu.VMEM((2, share, height, 128), F32),
            pltpu.SemaphoreType.DMA((share, 4)),
            pltpu.SemaphoreType.DMA((share, 4)),
            pltpu.SemaphoreType.DMA((peers,)),
            pltpu.SemaphoreType.DMA((peers,)),
            pltpu.SemaphoreType.DMA(()),
        ],
        compiler_params=pltpu.CompilerParams(vmem_limit_bytes=56 * MIB, collective_id=0, has_side_effects=True),
        cost_estimate=pl.CostEstimate(flops=60 * 10**9, bytes_accessed=200 * MIB, transcendentals=0),
        name="gram_terms",
    )((2 * refs).reshape(users * slots), table, values.astype(F32), weights)


def solve_kernel(packed, noise_cols, prior, shift, out, mats, right, back, sums):
    users = packed.shape[0]
    rank = prior.shape[0]
    half = rank // 2
    step = 32

    r, c = iota((half, half), 0), iota((half, half), 1)
    for m in range(users):
        both = packed[m, :half, :]
        cross = packed[m, half:rank, :]
        turned = both.T
        diag = packed[m, rank : rank + 1, :]
        first = jnp.where(r >= c, both, turned)
        last = jnp.where(r < c, both, jnp.where(r == c, diag, turned))
        mats[m, :half, :half] = prior[:half, :half] + ALPHA * first
        mats[m, :half, half:] = prior[:half, half:] + ALPHA * cross
        mats[m, half:, half:] = prior[half:, half:] + ALPHA * last
        right[m, 0:1, :half] = ALPHA * packed[m, rank + 1 : rank + 2, :] + shift[:, :half]
        right[m, 0:1, half:] = ALPHA * packed[m, rank + 2 : rank + 3, :] + shift[:, half:]

    sub = iota((1, 8, 128), 1)
    lane = iota((1, 8, 128), 2)
    tall_lane = iota((step, 128), 1)

    flat_lane = iota((8, 128), 1)

    def column(x, k):
        at = flat_lane // (2 * step) * (2 * step) + k
        return jnp.stack([jnp.take_along_axis(x[p], at, axis=1) for p in range(users // 2)])

    def later_work(m, k0, turn, rows, left, other):
        tile, group = k0 // half * half, k0 % half // step
        if not group:
            turn = pltpu.roll(turn, half - step, 1)
        keep = (tall_lane >= group * step) & (tall_lane < (group + 1) * step)
        turn = jnp.where(keep, turn, 0.0)
        back[m, k0 : k0 + step, :] = turn
        y = jnp.sum(turn * right[m, 0:1, tile : tile + half], axis=1, keepdims=True)
        right[m, 0:1, tile:] = right[m, 0:1, tile:] - jnp.sum(y * rows, axis=0, keepdims=True)
        sums[m, k0 : k0 + step, :] = jnp.broadcast_to(y + noise_cols[k0 : k0 + step, m : m + 1], (step, 128))
        low = k0 + 2 * step
        if low < rank:
            start = low // half * half
            change = dot_tn(left[:, start - tile :], other[:, start - tile :])
            mats[m, low:, start:] = mats[m, low:, start:] - change[low - start :]

    waiting = []
    for k0 in range(0, rank, step):
        tile, group = k0 // half * half, k0 % half // step
        parts, pivots = [], []
        for h in range(step // 8):
            rows = mats[:, k0 + 8 * h : k0 + 8 * h + 8, tile : tile + half]
            both = []
            for m in range(0, users, 2):
                turns = [(half - group * step) % half, (half + 2 * step - group * step) % half]
                one, two = [pltpu.roll(rows[m + e], turns[e], 1) if turns[e] else rows[m + e] for e in range(2)]
                both.append(jnp.where(lane[0] < 2 * step, one, two))
            unit = jnp.where(lane % step == sub + 8 * h, 1.0, 0.0)
            parts.append(jnp.where(lane % (2 * step) < step, jnp.stack(both), unit))
            pivots.append(jnp.ones((users // 2, 8, 128), F32))
        for k in range(0, step, 2):
            f, kk = k // 8, k % 8
            ones = [column(parts[h], k) for h in range(f, step // 8)]
            twos = [column(parts[h], k + 1) for h in range(f, step // 8)]
            a, b, c = ones[0][:, kk : kk + 1, :], twos[0][:, kk : kk + 1, :], twos[0][:, kk + 1 : kk + 2, :]
            low, high = parts[f][:, kk : kk + 1, :], parts[f][:, kk + 1 : kk + 2, :]
            inv = 1.0 / (a * c - b * b)
            ratio = b * (1.0 / a)
            first = (c * low - b * high) * inv
            second = (a * high - b * low) * inv
            second_row = parts[f] - ratio * low
            pivots[f] = jnp.where(sub == kk, a, jnp.where(sub == kk + 1, c - ratio * b, pivots[f]))
            for h in range(f, step // 8):
                new = parts[h] - ones[h - f] * first - twos[h - f] * second
                if h == f:
                    new = jnp.where(sub > kk + 1, new, jnp.where(sub == kk + 1, second_row, parts[h]))
                parts[h] = new
            if waiting:
                later_work(*waiting.pop(0))
        while waiting:
            later_work(*waiting.pop(0))
        scaled = [p * lax.rsqrt(v) for p, v in zip(parts, pivots)]
        for m in range(users):
            turn = jnp.concatenate([x[m // 2] for x in scaled], axis=0)
            at = (m % 2) * 2 * step + step
            turn = jnp.where((tall_lane >= at) & (tall_lane < at + step), turn, 0.0)
            ways = (step, 2 * step) if m % 2 == 0 else (2 * step, 3 * step)
            turn = turn + pltpu.roll(turn, ways[0], 1) + pltpu.roll(turn, ways[1], 1)
            hi, mid, low = split3(turn)
            one = jnp.where(tall_lane < step, 0.0, jnp.where(tall_lane < 3 * step, hi, mid))
            two = jnp.where(tall_lane < step, 0.0, jnp.where(tall_lane < 2 * step, hi, jnp.where(tall_lane < 3 * step, low, mid)))
            left = jnp.concatenate([one, two], axis=1).astype(BF16)
            hi, mid, low = split3(mats[m, k0 : k0 + step, tile:])
            other = jnp.concatenate([hi, hi, mid, hi, hi, low, hi, mid], axis=0).astype(BF16)
            rows = jnp.dot(left, other, preferred_element_type=F32)
            mats[m, k0 : k0 + step, tile:] = rows
            near = k0 + step
            left, other = stacked3(rows)
            if near < rank:
                start = near // half * half
                change = dot_tn(left[:, start - tile : start - tile + half], other[:, start - tile :])
                change = change[near - start : near - start + step]
                mats[m, near : near + step, start:] = mats[m, near : near + step, start:] - change
            waiting.append((m, k0, turn, rows, left, other))
    while waiting:
        later_work(*waiting.pop(0))

    x = [jnp.zeros((users, 1, half), F32)] * 2
    for k0 in range(rank - step, -1, -step):
        t = k0 // half
        at = pl.ds(k0, step)
        part = mats[:, at, half:] * x[1]
        if t == 0:
            part = part + mats[:, at, :half] * x[0]
        rest = sums[:, at, :] - jnp.sum(part, axis=2, keepdims=True)
        x[t] = x[t] + jnp.sum(back[:, at, :] * rest, axis=1, keepdims=True)
    for m in range(users):
        out[m : m + 1, :half] = x[0][m]
        out[m : m + 1, half:] = x[1][m]


def solve_users(packed, noise, prior, shift):
    users = packed.shape[0]
    rank = prior.shape[0]
    vmem = pl.BlockSpec(memory_space=pltpu.VMEM)
    return pl.pallas_call(
        solve_kernel,
        in_specs=[vmem] * 4,
        out_specs=vmem,
        out_shape=jax.ShapeDtypeStruct((users, rank), F32),
        scratch_shapes=[
            pltpu.VMEM((users, rank, rank), F32),
            pltpu.VMEM((users, 8, rank), F32),
            pltpu.VMEM((users, rank, 128), F32),
            pltpu.VMEM((users, rank, 128), F32),
        ],
        compiler_params=pltpu.CompilerParams(vmem_limit_bytes=48 * MIB),
        name="solve_users",
    )(packed, noise.T, prior, shift.reshape(1, rank))


def share_kernel(own, out, first_send, first_recv, send_sem, recv_sem, twin_send, twin_recv):
    g, u = lax.axis_index("grp"), lax.axis_index("usr")
    ring, side = 4, 4
    core, x, z = u % 2, u // 2 % side, u // (2 * side)
    twin = u + 1 - 2 * core
    moves = [(a, b) for a in range(side) for b in range(side) if a or b]

    def place(dz, dx):
        return (z + dz) % side * (2 * side) + (x + dx) % side * 2 + core

    barrier = pltpu.get_barrier_semaphore()
    for o in range(1, ring):
        pl.semaphore_signal(barrier, inc=1, device_id={"grp": (g + o) % ring}, device_id_type=MESH)
    for move in moves:
        pl.semaphore_signal(barrier, inc=1, device_id={"usr": place(*move)}, device_id_type=MESH)
    pl.semaphore_signal(barrier, inc=1, device_id={"usr": twin}, device_id_type=MESH)
    pl.semaphore_wait(barrier, ring + len(moves))

    def remote(src, dst, send, recv, peer):
        return pltpu.make_async_remote_copy(
            src_ref=src, dst_ref=dst, send_sem=send, recv_sem=recv, device_id=peer, device_id_type=MESH
        )

    first = [
        remote(own, out.at[u, g], first_send.at[o - 1], first_recv.at[o - 1], {"grp": (g + o) % ring})
        for o in range(1, ring)
    ]
    for c in first:
        c.start()
    out[u, g] = own[...]
    for o in range(1, ring):
        src = (g + ring - o) % ring
        remote(own, out.at[u, src], first_send.at[o - 1], first_recv.at[o - 1], {"grp": src}).wait_recv()
    slab = out.at[u]
    second = [
        remote(slab, slab, send_sem.at[k], recv_sem.at[k], {"usr": place(*move)}) for k, move in enumerate(moves)
    ]
    for c in second:
        c.start()
    to_twin = [remote(slab, slab, twin_send.at[len(moves)], twin_recv.at[len(moves)], {"usr": twin})]
    to_twin[0].start()
    for k, (dz, dx) in enumerate(moves):
        src = out.at[place(-dz + side, -dx + side)]
        remote(src, src, send_sem.at[k], recv_sem.at[k], {"usr": twin}).wait_recv()
        c = remote(src, src, twin_send.at[k], twin_recv.at[k], {"usr": twin})
        c.start()
        to_twin.append(c)
    for c in to_twin:
        c.wait_recv()
    for c in first + second + to_twin:
        c.wait_send()


def share_samples(own):
    share, rank = own.shape
    peers, ring = lax.axis_size("usr"), lax.axis_size("grp")
    vmem = pl.BlockSpec(memory_space=pltpu.VMEM)
    dma = pltpu.SemaphoreType.DMA
    return pl.pallas_call(
        share_kernel,
        in_specs=[vmem],
        out_specs=vmem,
        out_shape=jax.ShapeDtypeStruct((peers, ring, share, rank), F32),
        scratch_shapes=[dma((ring - 1,)), dma((ring - 1,)), dma((15,)), dma((15,)), dma((16,)), dma((16,))],
        compiler_params=pltpu.CompilerParams(vmem_limit_bytes=32 * MIB, collective_id=1, has_side_effects=True),
        name="share_samples",
    )(own)


def stats_kernel(cols, listed, live, weights, samples, out, held):
    out[...] = jnp.zeros_like(out)
    parts, share = samples.shape[1:3]
    unroll = 4

    def device(d):
        for g in range(parts):
            held[g * share : (g + 1) * share, :] = samples[d, g]
        hi, lo = split(held[...])
        other = jnp.concatenate([hi, lo, hi], axis=0).astype(BF16)
        terms = []
        for c in range(cols):
            hi, lo = split(jnp.where(live[d * cols + c] > 0, ALPHA * weights[d * cols + c], 0.0))
            left = jnp.concatenate([hi, hi, lo], axis=0).astype(BF16)
            terms.append(dot_tn(left, other))
        for c in range(cols):
            b = listed[d * cols + c]
            out[b] = out[b] + terms[c]

    def devices(i, carry):
        for e in range(unroll):
            device(unroll * i + e)
        return carry

    lax.fori_loop(0, samples.shape[0] // unroll, devices, 0)


def make_stats(weights, samples, listed, live, owned):
    n, users, height = weights.shape
    peers, _, _, rank = samples.shape
    vmem = pl.BlockSpec(memory_space=pltpu.VMEM)
    smem = pl.BlockSpec(memory_space=pltpu.SMEM)
    return pl.pallas_call(
        functools.partial(stats_kernel, n // peers),
        in_specs=[smem, smem, vmem, vmem],
        out_specs=vmem,
        out_shape=jax.ShapeDtypeStruct((owned, height, rank), F32),
        scratch_shapes=[pltpu.VMEM((users, rank), F32)],
        compiler_params=pltpu.CompilerParams(vmem_limit_bytes=32 * MIB),
        name="make_stats",
    )(listed, live, weights, samples)


def on_device(item_factors, send_ids, send_count, rating_pointer, rating_value, noise, prior_prec, prior_shift):
    peers = lax.axis_size("usr")
    blocks = item_factors[0]
    owned, height, rank = blocks.shape
    cols = send_ids.shape[-1]
    n = peers * cols
    listed = send_ids[0, 0].reshape(n)
    live = (jnp.arange(cols, dtype=jnp.int32)[None, :] < send_count[0, 0][:, None]).astype(jnp.int32).reshape(n)
    refs, values = rating_pointer[0], rating_value[0]

    outgoing = pick_blocks(blocks, listed, live)
    incoming = lax.all_to_all(outgoing, "usr", split_axis=0, concat_axis=0, tiled=True)
    weights = make_weights(refs, values, n, height)
    packed, gathered = gram_terms(incoming.reshape(n * height, rank), refs, values, weights)
    share = packed.shape[0]
    draws = lax.dynamic_slice_in_dim(noise, lax.axis_index("grp") * share, share, 0)
    everyone = share_samples(solve_users(packed, draws, prior_prec, prior_shift))
    samples = lax.dynamic_index_in_dim(everyone, lax.axis_index("usr"), 0, keepdims=False)
    samples = samples.reshape(refs.shape[0], rank)
    stats = make_stats(gathered, everyone, listed, live, owned)
    return (samples, stats[None])


def solution(mesh):
    placed = (
        P("grp", "usr", None, None),
        P("grp", "usr", None, None),
        P("grp", "usr", None),
        P("grp", "usr", None),
        P("grp", "usr", None),
        P("usr", None),
        P(),
        P(),
    )
    return jax.shard_map(
        on_device,
        mesh=mesh,
        in_specs=placed,
        out_specs=(P("usr", None), P("grp", "usr", None, None)),
        check_vma=False,
    )
```

```python
import functools

import jax
import jax.numpy as jnp
from jax import lax
from jax.experimental import pallas as pl
from jax.experimental.pallas import tpu as pltpu
from jax.sharding import PartitionSpec as P

ALPHA = 2.0
F32 = jnp.float32
BF16 = jnp.bfloat16
MIB = 2**20
MESH = pl.DeviceIdType.MESH


def iota(shape, dim):
    return lax.broadcasted_iota(jnp.int32, shape, dim)


def split(x):
    hi = x.astype(BF16).astype(F32)
    return hi, x - hi


def split3(x):
    hi = x.astype(BF16).astype(F32)
    rest = x - hi
    mid = rest.astype(BF16).astype(F32)
    return hi, mid, rest - mid


def stacked3(x):
    hi, mid, low = split3(x)
    left = jnp.concatenate([hi, hi, mid, hi, low, mid], axis=0).astype(BF16)
    right = jnp.concatenate([hi, mid, hi, low, hi, mid], axis=0).astype(BF16)
    return left, right


def dot_tn(a, b):
    return lax.dot_general(a, b, (((0,), (0,)), ((), ())), preferred_element_type=F32)


def pick_kernel(cols, per_step, listed, live, blocks, out):
    base = pl.program_id(0) * per_step

    def body(i, carry):
        keep = live[base + i] > 0
        block = blocks[listed[base + i]]
        out[i] = jnp.where(keep, block, jnp.zeros_like(block))
        return carry

    lax.fori_loop(0, per_step, body, 0)


def pick_blocks(blocks, listed, live):
    n = listed.shape[0]
    owned, height, rank = blocks.shape
    steps = 4
    per_step = n // steps
    return pl.pallas_call(
        functools.partial(pick_kernel, n, per_step),
        grid_spec=pltpu.PrefetchScalarGridSpec(
            num_scalar_prefetch=2,
            grid=(steps,),
            in_specs=[pl.BlockSpec((owned, height, rank), lambda s, *_: (0, 0, 0))],
            out_specs=pl.BlockSpec((per_step, height, rank), lambda s, *_: (s, 0, 0)),
        ),
        out_shape=jax.ShapeDtypeStruct((n, height, rank), BF16),
        compiler_params=pltpu.CompilerParams(vmem_limit_bytes=32 * MIB),
        name="pick_blocks",
    )(listed, live, blocks)


def weight_kernel(refs, values, out):
    n_blocks, users, height = out.shape
    slots = refs.shape[1]
    for u in range(users):
        ref = refs[u : u + 1, :]
        value = values[u : u + 1, :].astype(F32)
        block = ref // height
        row = ref % height
        hot_block = jnp.where(iota((n_blocks, slots), 0) == block, value, 0.0).astype(BF16)
        hot_row = jnp.where(iota((height, slots), 0) == row, 1.0, 0.0).astype(BF16)
        out[:, u, :] = lax.dot_general(hot_block, hot_row, (((1,), (1,)), ((), ())), preferred_element_type=F32)


def make_weights(refs, values, n_blocks, height):
    users, slots = refs.shape
    group = 8
    return pl.pallas_call(
        weight_kernel,
        grid=(users // group,),
        in_specs=[pl.BlockSpec((group, slots), lambda i: (i, 0))] * 2,
        out_specs=pl.BlockSpec((n_blocks, group, height), lambda i: (0, i, 0)),
        out_shape=jax.ShapeDtypeStruct((n_blocks, users, height), F32),
        compiler_params=pltpu.CompilerParams(vmem_limit_bytes=32 * MIB),
        name="make_weights",
    )(refs, values)


def gather_rows(wide, picked, refs, user):
    slots = picked.shape[0] // 2
    unroll = 16
    for base in range(0, slots, unroll):
        got = [wide[pl.ds(refs[user * slots + base + j], 2), :] for j in range(unroll)]
        for j in range(unroll):
            picked[2 * (base + j) : 2 * (base + j) + 2, :] = got[j]


def packed_terms(picked, value, store):
    slots = picked.shape[0] // 2
    low = picked[pl.ds(0, slots, stride=2), :].astype(BF16)
    high = picked[pl.ds(1, slots, stride=2), :].astype(BF16)
    mat = jnp.concatenate([low, high], axis=1)
    gram = dot_tn(mat, mat)
    linear = lax.dot_general(
        jnp.broadcast_to(value, (8, slots)), mat, (((1,), (0,)), ((), ())), preferred_element_type=F32
    )
    r, c = iota((128, 128), 0), iota((128, 128), 1)
    last = gram[128:, 128:]
    store(0, jnp.where(r >= c, gram[:128, :128], last))
    store(128, gram[:128, 128:])
    diag = jnp.sum(jnp.where(r == c, last, 0.0), axis=0, keepdims=True)
    row = iota((8, 128), 0)
    tail = jnp.where(row == 1, linear[:, :128], jnp.where(row == 2, linear[:, 128:], 0.0))
    store(256, jnp.where(row == 0, diag, tail))


def gram_kernel(
    refs, table, values, weights, out, gathered, wide, even, odd, stage, near, far, send_sem, recv_sem, give_sem, take_sem, own_sem
):
    rows = table.shape[0]
    share, height, _ = out.shape
    chunk, cut = 128, near.shape[2] // 16 * 8
    me, ring = lax.axis_index("grp"), 4
    after, before = (me + 1) % ring, (me + ring - 1) % ring
    u, peers = lax.axis_index("usr"), lax.axis_size("usr")
    cols = weights.shape[0] // peers

    barrier = pltpu.get_barrier_semaphore()
    for peer in (after, before):
        pl.semaphore_signal(barrier, inc=1, device_id={"grp": peer}, device_id_type=MESH)
    for o in range(1, peers):
        pl.semaphore_signal(barrier, inc=1, device_id={"usr": (u + o) % peers}, device_id_type=MESH)

    def give(o):
        peer = (u + o) % peers
        return pltpu.make_async_remote_copy(
            src_ref=weights.at[pl.ds(peer * cols, cols)],
            dst_ref=gathered.at[pl.ds(u * cols, cols)],
            send_sem=give_sem.at[o],
            recv_sem=take_sem.at[o],
            device_id={"usr": peer},
            device_id_type=MESH,
        )

    def take(o):
        peer = (u + peers - o) % peers
        slab = gathered.at[pl.ds(peer * cols, cols)]
        return pltpu.make_async_remote_copy(
            src_ref=slab,
            dst_ref=slab,
            send_sem=give_sem.at[o],
            recv_sem=take_sem.at[o],
            device_id={"usr": peer},
            device_id_type=MESH,
        )

    def widen(i, carry):
        part = table[pl.ds(i * chunk, chunk), :].astype(F32)
        wide[pl.ds(i * 2 * chunk, chunk, stride=2), :] = part[:, :128]
        wide[pl.ds(i * 2 * chunk + 1, chunk, stride=2), :] = part[:, 128:]
        return carry

    lax.fori_loop(0, rows // chunk, widen, 0)
    pl.semaphore_wait(barrier, peers + 1)

    keep = pltpu.make_async_copy(
        weights.at[pl.ds(u * cols, cols)], gathered.at[pl.ds(u * cols, cols)], own_sem
    )
    keep.start()

    def send_weights(o, carry):
        give(o).start()
        return carry

    lax.fori_loop(1, peers, send_weights, 0)

    def copy(j, kind):
        if kind == 0:
            src, dst, peer = stage.at[2, j, :cut], far.at[0, j, :cut], after
        elif kind == 1:
            src, dst, peer = stage.at[2, j, cut:], far.at[1, j, cut:], before
        elif kind == 2:
            src, dst, peer = stage.at[1, j], near.at[0, j], after
        else:
            src, dst, peer = stage.at[3, j], near.at[1, j], before
        return pltpu.make_async_remote_copy(
            src_ref=src,
            dst_ref=dst,
            send_sem=send_sem.at[j, kind],
            recv_sem=recv_sem.at[j, kind],
            device_id={"grp": peer},
            device_id_type=MESH,
        )

    def user(j, kind):
        return (me + kind) % ring * share + j

    def terms(picked, j, kind):
        def store(at, part):
            stage[kind, j, at : at + part.shape[0], :] = part

        packed_terms(picked, values[pl.ds(user(j, kind), 1), :].astype(BF16), store)

    def pass_on(j):
        copy(j, 0).wait_recv()
        stage[1, j, :cut, :] = stage[1, j, :cut, :] + far[0, j, :cut, :]
        copy(j, 2).start()
        copy(j, 1).wait_recv()
        stage[3, j, cut:, :] = stage[3, j, cut:, :] + far[1, j, cut:, :]
        copy(j, 3).start()

    def finish(j):
        copy(j, 2).wait_recv()
        copy(j, 3).wait_recv()
        out[j] = stage[0, j] + near[0, j] + near[1, j]

    gather_rows(wide, even, refs, user(0, 2))

    def furthest(i, carry):
        gather_rows(wide, odd, refs, user(2 * i + 1, 2))
        terms(even, 2 * i, 2)
        copy(2 * i, 0).start()
        copy(2 * i, 1).start()
        following = 2 * i + 2
        gather_rows(wide, even, refs, user(following % share, 2 - following // share))
        terms(odd, 2 * i + 1, 2)
        copy(2 * i + 1, 0).start()
        copy(2 * i + 1, 1).start()
        return carry

    lax.fori_loop(0, share // 2, furthest, 0)

    def neighbours(j, carry):
        gather_rows(wide, odd, refs, user(j, 3))
        terms(even, j, 1)
        following = j + 1
        gather_rows(wide, even, refs, user(following % share, 1 - following // share))
        terms(odd, j, 3)
        pass_on(j)
        return carry

    lax.fori_loop(0, share, neighbours, 0)

    def own_terms(i, carry):
        gather_rows(wide, odd, refs, user(2 * i + 1, 0))
        terms(even, 2 * i, 0)
        gather_rows(wide, even, refs, user((2 * i + 2) % share, 0))
        terms(odd, 2 * i + 1, 0)
        return carry

    lax.fori_loop(0, share // 2, own_terms, 0)

    def finish_all(j, carry):
        finish(j)
        return carry

    lax.fori_loop(0, share, finish_all, 0)

    def drain(j, carry):
        for kind in range(4):
            copy(j, kind).wait_send()
        return carry

    lax.fori_loop(0, share, drain, 0)

    def drain_weights(o, carry):
        give(o).wait_send()
        take(o).wait_recv()
        return carry

    lax.fori_loop(1, peers, drain_weights, 0)
    keep.wait()


def gram_terms(table, refs, values, weights):
    users, slots = refs.shape
    rows, rank = table.shape
    ring, height = 4, 264
    share = users // ring
    peers = lax.axis_size("usr")
    vmem = pl.BlockSpec(memory_space=pltpu.VMEM)
    hbm = pl.BlockSpec(memory_space=pltpu.HBM)
    return pl.pallas_call(
        gram_kernel,
        in_specs=[pl.BlockSpec(memory_space=pltpu.SMEM), vmem, vmem, hbm],
        out_specs=(vmem, hbm),
        out_shape=(
            jax.ShapeDtypeStruct((share, height, 128), F32),
            jax.ShapeDtypeStruct(weights.shape, F32),
        ),
        scratch_shapes=[
            pltpu.VMEM((2 * rows, 128), F32),
            pltpu.VMEM((2 * slots, 128), F32),
            pltpu.VMEM((2 * slots, 128), F32),
            pltpu.VMEM((ring, share, height, 128), F32),
            pltpu.VMEM((2, share, height, 128), F32),
            pltpu.VMEM((2, share, height, 128), F32),
            pltpu.SemaphoreType.DMA((share, 4)),
            pltpu.SemaphoreType.DMA((share, 4)),
            pltpu.SemaphoreType.DMA((peers,)),
            pltpu.SemaphoreType.DMA((peers,)),
            pltpu.SemaphoreType.DMA(()),
        ],
        compiler_params=pltpu.CompilerParams(vmem_limit_bytes=56 * MIB, collective_id=0, has_side_effects=True),
        cost_estimate=pl.CostEstimate(flops=60 * 10**9, bytes_accessed=200 * MIB, transcendentals=0),
        name="gram_terms",
    )((2 * refs).reshape(users * slots), table, values.astype(F32), weights)


def solve_kernel(packed, noise_cols, prior, shift, out, mats, right, back, sums):
    users = packed.shape[0]
    rank = prior.shape[0]
    half = rank // 2
    step = 32

    r, c = iota((half, half), 0), iota((half, half), 1)
    for m in range(users):
        both = packed[m, :half, :]
        cross = packed[m, half:rank, :]
        turned = both.T
        diag = packed[m, rank : rank + 1, :]
        first = jnp.where(r >= c, both, turned)
        last = jnp.where(r < c, both, jnp.where(r == c, diag, turned))
        mats[m, :half, :half] = prior[:half, :half] + ALPHA * first
        mats[m, :half, half:] = prior[:half, half:] + ALPHA * cross
        mats[m, half:, half:] = prior[half:, half:] + ALPHA * last
        right[m, 0:1, :half] = ALPHA * packed[m, rank + 1 : rank + 2, :] + shift[:, :half]
        right[m, 0:1, half:] = ALPHA * packed[m, rank + 2 : rank + 3, :] + shift[:, half:]

    sub = iota((1, 8, 128), 1)
    lane = iota((1, 8, 128), 2)
    tall_lane = iota((step, 128), 1)

    flat_lane = iota((8, 128), 1)

    def column(x, k):
        at = flat_lane // (2 * step) * (2 * step) + k
        return jnp.stack([jnp.take_along_axis(x[p], at, axis=1) for p in range(users // 2)])

    def later_work(m, k0, turn, rows, left, other):
        tile, group = k0 // half * half, k0 % half // step
        if not group:
            turn = pltpu.roll(turn, half - step, 1)
        keep = (tall_lane >= group * step) & (tall_lane < (group + 1) * step)
        turn = jnp.where(keep, turn, 0.0)
        back[m, k0 : k0 + step, :] = turn
        y = jnp.sum(turn * right[m, 0:1, tile : tile + half], axis=1, keepdims=True)
        right[m, 0:1, tile:] = right[m, 0:1, tile:] - jnp.sum(y * rows, axis=0, keepdims=True)
        sums[m, k0 : k0 + step, :] = jnp.broadcast_to(y + noise_cols[k0 : k0 + step, m : m + 1], (step, 128))
        low = k0 + 2 * step
        if low < rank:
            start = low // half * half
            change = dot_tn(left[:, start - tile :], other[:, start - tile :])
            mats[m, low:, start:] = mats[m, low:, start:] - change[low - start :]

    waiting = []
    for k0 in range(0, rank, step):
        tile, group = k0 // half * half, k0 % half // step
        parts, pivots = [], []
        for h in range(step // 8):
            rows = mats[:, k0 + 8 * h : k0 + 8 * h + 8, tile : tile + half]
            both = []
            for m in range(0, users, 2):
                turns = [(half - group * step) % half, (half + 2 * step - group * step) % half]
                one, two = [pltpu.roll(rows[m + e], turns[e], 1) if turns[e] else rows[m + e] for e in range(2)]
                both.append(jnp.where(lane[0] < 2 * step, one, two))
            unit = jnp.where(lane % step == sub + 8 * h, 1.0, 0.0)
            parts.append(jnp.where(lane % (2 * step) < step, jnp.stack(both), unit))
            pivots.append(jnp.ones((users // 2, 8, 128), F32))
        for k in range(0, step, 2):
            f, kk = k // 8, k % 8
            ones = [column(parts[h], k) for h in range(f, step // 8)]
            twos = [column(parts[h], k + 1) for h in range(f, step // 8)]
            a, b, c = ones[0][:, kk : kk + 1, :], twos[0][:, kk : kk + 1, :], twos[0][:, kk + 1 : kk + 2, :]
            low, high = parts[f][:, kk : kk + 1, :], parts[f][:, kk + 1 : kk + 2, :]
            inv = 1.0 / (a * c - b * b)
            ratio = b * (1.0 / a)
            first = (c * low - b * high) * inv
            second = (a * high - b * low) * inv
            second_row = parts[f] - ratio * low
            pivots[f] = jnp.where(sub == kk, a, jnp.where(sub == kk + 1, c - ratio * b, pivots[f]))
            for h in range(f, step // 8):
                new = parts[h] - ones[h - f] * first - twos[h - f] * second
                if h == f:
                    new = jnp.where(sub > kk + 1, new, jnp.where(sub == kk + 1, second_row, parts[h]))
                parts[h] = new
            if waiting:
                later_work(*waiting.pop(0))
        while waiting:
            later_work(*waiting.pop(0))
        scaled = [p * lax.rsqrt(v) for p, v in zip(parts, pivots)]
        for m in range(users):
            turn = jnp.concatenate([x[m // 2] for x in scaled], axis=0)
            at = (m % 2) * 2 * step + step
            turn = jnp.where((tall_lane >= at) & (tall_lane < at + step), turn, 0.0)
            ways = (step, 2 * step) if m % 2 == 0 else (2 * step, 3 * step)
            turn = turn + pltpu.roll(turn, ways[0], 1) + pltpu.roll(turn, ways[1], 1)
            hi, mid, low = split3(turn)
            one = jnp.where(tall_lane < step, 0.0, jnp.where(tall_lane < 3 * step, hi, mid))
            two = jnp.where(tall_lane < step, 0.0, jnp.where(tall_lane < 2 * step, hi, jnp.where(tall_lane < 3 * step, low, mid)))
            left = jnp.concatenate([one, two], axis=1).astype(BF16)
            hi, mid, low = split3(mats[m, k0 : k0 + step, tile:])
            other = jnp.concatenate([hi, hi, mid, hi, hi, low, hi, mid], axis=0).astype(BF16)
            rows = jnp.dot(left, other, preferred_element_type=F32)
            mats[m, k0 : k0 + step, tile:] = rows
            near = k0 + step
            left, other = stacked3(rows)
            if near < rank:
                start = near // half * half
                change = dot_tn(left[:, start - tile : start - tile + half], other[:, start - tile :])
                change = change[near - start : near - start + step]
                mats[m, near : near + step, start:] = mats[m, near : near + step, start:] - change
            waiting.append((m, k0, turn, rows, left, other))
    while waiting:
        later_work(*waiting.pop(0))

    x = [jnp.zeros((users, 1, half), F32)] * 2
    for k0 in range(rank - step, -1, -step):
        t = k0 // half
        at = pl.ds(k0, step)
        part = mats[:, at, half:] * x[1]
        if t == 0:
            part = part + mats[:, at, :half] * x[0]
        rest = sums[:, at, :] - jnp.sum(part, axis=2, keepdims=True)
        x[t] = x[t] + jnp.sum(back[:, at, :] * rest, axis=1, keepdims=True)
    for m in range(users):
        out[m : m + 1, :half] = x[0][m]
        out[m : m + 1, half:] = x[1][m]


def solve_users(packed, noise, prior, shift):
    users = packed.shape[0]
    rank = prior.shape[0]
    vmem = pl.BlockSpec(memory_space=pltpu.VMEM)
    return pl.pallas_call(
        solve_kernel,
        in_specs=[vmem] * 4,
        out_specs=vmem,
        out_shape=jax.ShapeDtypeStruct((users, rank), F32),
        scratch_shapes=[
            pltpu.VMEM((users, rank, rank), F32),
            pltpu.VMEM((users, 8, rank), F32),
            pltpu.VMEM((users, rank, 128), F32),
            pltpu.VMEM((users, rank, 128), F32),
        ],
        compiler_params=pltpu.CompilerParams(vmem_limit_bytes=48 * MIB),
        name="solve_users",
    )(packed, noise.T, prior, shift.reshape(1, rank))


def share_kernel(own, out, first_send, first_recv, send_sem, recv_sem, twin_send, twin_recv):
    g, u = lax.axis_index("grp"), lax.axis_index("usr")
    ring, side = 4, 4
    core, x, z = u % 2, u // 2 % side, u // (2 * side)
    twin = u + 1 - 2 * core
    moves = [(a, b) for a in range(side) for b in range(side) if a or b]

    def place(dz, dx):
        return (z + dz) % side * (2 * side) + (x + dx) % side * 2 + core

    barrier = pltpu.get_barrier_semaphore()
    for o in range(1, ring):
        pl.semaphore_signal(barrier, inc=1, device_id={"grp": (g + o) % ring}, device_id_type=MESH)
    for move in moves:
        pl.semaphore_signal(barrier, inc=1, device_id={"usr": place(*move)}, device_id_type=MESH)
    pl.semaphore_signal(barrier, inc=1, device_id={"usr": twin}, device_id_type=MESH)
    pl.semaphore_wait(barrier, ring + len(moves))

    def remote(src, dst, send, recv, peer):
        return pltpu.make_async_remote_copy(
            src_ref=src, dst_ref=dst, send_sem=send, recv_sem=recv, device_id=peer, device_id_type=MESH
        )

    first = [
        remote(own, out.at[u, g], first_send.at[o - 1], first_recv.at[o - 1], {"grp": (g + o) % ring})
        for o in range(1, ring)
    ]
    for c in first:
        c.start()
    out[u, g] = own[...]
    for o in range(1, ring):
        src = (g + ring - o) % ring
        remote(own, out.at[u, src], first_send.at[o - 1], first_recv.at[o - 1], {"grp": src}).wait_recv()
    slab = out.at[u]
    second = [
        remote(slab, slab, send_sem.at[k], recv_sem.at[k], {"usr": place(*move)}) for k, move in enumerate(moves)
    ]
    for c in second:
        c.start()
    to_twin = [remote(slab, slab, twin_send.at[len(moves)], twin_recv.at[len(moves)], {"usr": twin})]
    to_twin[0].start()
    for k, (dz, dx) in enumerate(moves):
        src = out.at[place(-dz + side, -dx + side)]
        remote(src, src, send_sem.at[k], recv_sem.at[k], {"usr": twin}).wait_recv()
        c = remote(src, src, twin_send.at[k], twin_recv.at[k], {"usr": twin})
        c.start()
        to_twin.append(c)
    for c in to_twin:
        c.wait_recv()
    for c in first + second + to_twin:
        c.wait_send()


def share_samples(own):
    share, rank = own.shape
    peers, ring = lax.axis_size("usr"), lax.axis_size("grp")
    vmem = pl.BlockSpec(memory_space=pltpu.VMEM)
    dma = pltpu.SemaphoreType.DMA
    return pl.pallas_call(
        share_kernel,
        in_specs=[vmem],
        out_specs=vmem,
        out_shape=jax.ShapeDtypeStruct((peers, ring, share, rank), F32),
        scratch_shapes=[dma((ring - 1,)), dma((ring - 1,)), dma((15,)), dma((15,)), dma((16,)), dma((16,))],
        compiler_params=pltpu.CompilerParams(vmem_limit_bytes=32 * MIB, collective_id=1, has_side_effects=True),
        name="share_samples",
    )(own)


def stats_kernel(cols, listed, live, weights, samples, out, held):
    out[...] = jnp.zeros_like(out)
    parts, share = samples.shape[1:3]
    unroll = 4

    def device(d):
        for g in range(parts):
            held[g * share : (g + 1) * share, :] = samples[d, g]
        hi, lo = split(held[...])
        other = jnp.concatenate([hi, lo, hi], axis=0).astype(BF16)
        terms = []
        for c in range(cols):
            hi, lo = split(jnp.where(live[d * cols + c] > 0, ALPHA * weights[d * cols + c], 0.0))
            left = jnp.concatenate([hi, hi, lo], axis=0).astype(BF16)
            terms.append(dot_tn(left, other))
        for c in range(cols):
            b = listed[d * cols + c]
            out[b] = out[b] + terms[c]

    def devices(i, carry):
        for e in range(unroll):
            device(unroll * i + e)
        return carry

    lax.fori_loop(0, samples.shape[0] // unroll, devices, 0)


def make_stats(weights, samples, listed, live, owned):
    n, users, height = weights.shape
    peers, _, _, rank = samples.shape
    vmem = pl.BlockSpec(memory_space=pltpu.VMEM)
    smem = pl.BlockSpec(memory_space=pltpu.SMEM)
    return pl.pallas_call(
        functools.partial(stats_kernel, n // peers),
        in_specs=[smem, smem, vmem, vmem],
        out_specs=vmem,
        out_shape=jax.ShapeDtypeStruct((owned, height, rank), F32),
        scratch_shapes=[pltpu.VMEM((users, rank), F32)],
        compiler_params=pltpu.CompilerParams(vmem_limit_bytes=32 * MIB),
        name="make_stats",
    )(listed, live, weights, samples)


def on_device(item_factors, send_ids, send_count, rating_pointer, rating_value, noise, prior_prec, prior_shift):
    peers = lax.axis_size("usr")
    blocks = item_factors[0]
    owned, height, rank = blocks.shape
    cols = send_ids.shape[-1]
    n = peers * cols
    listed = send_ids[0, 0].reshape(n)
    live = (jnp.arange(cols, dtype=jnp.int32)[None, :] < send_count[0, 0][:, None]).astype(jnp.int32).reshape(n)
    refs, values = rating_pointer[0], rating_value[0]

    outgoing = pick_blocks(blocks, listed, live)
    incoming = lax.all_to_all(outgoing, "usr", split_axis=0, concat_axis=0, tiled=True)
    weights = make_weights(refs, values, n, height)
    packed, gathered = gram_terms(incoming.reshape(n * height, rank), refs, values, weights)
    share = packed.shape[0]
    draws = lax.dynamic_slice_in_dim(noise, lax.axis_index("grp") * share, share, 0)
    everyone = share_samples(solve_users(packed, draws, prior_prec, prior_shift))
    samples = lax.dynamic_index_in_dim(everyone, lax.axis_index("usr"), 0, keepdims=False)
    samples = samples.reshape(refs.shape[0], rank)
    stats = make_stats(gathered, everyone, listed, live, owned)
    return (samples, stats[None])


def solution(mesh):
    placed = (
        P("grp", "usr", None, None),
        P("grp", "usr", None, None),
        P("grp", "usr", None),
        P("grp", "usr", None),
        P("grp", "usr", None),
        P("usr", None),
        P(),
        P(),
    )
    return jax.shard_map(
        on_device,
        mesh=mesh,
        in_specs=placed,
        out_specs=(P("usr", None), P("grp", "usr", None, None)),
        check_vma=False,
    )
```

```python
import functools

import jax
import jax.numpy as jnp
from jax import lax
from jax.experimental import pallas as pl
from jax.experimental.pallas import tpu as pltpu
from jax.sharding import PartitionSpec as P

ALPHA = 2.0
F32 = jnp.float32
BF16 = jnp.bfloat16
MIB = 2**20
MESH = pl.DeviceIdType.MESH


def iota(shape, dim):
    return lax.broadcasted_iota(jnp.int32, shape, dim)


def split(x):
    hi = x.astype(BF16).astype(F32)
    return hi, x - hi


def split3(x):
    hi = x.astype(BF16).astype(F32)
    rest = x - hi
    mid = rest.astype(BF16).astype(F32)
    return hi, mid, rest - mid


def stacked3(x):
    hi, mid, low = split3(x)
    left = jnp.concatenate([hi, hi, mid, hi, low, mid], axis=0).astype(BF16)
    right = jnp.concatenate([hi, mid, hi, low, hi, mid], axis=0).astype(BF16)
    return left, right


def dot_tn(a, b):
    return lax.dot_general(a, b, (((0,), (0,)), ((), ())), preferred_element_type=F32)


def pick_kernel(cols, per_step, listed, live, blocks, out):
    base = pl.program_id(0) * per_step

    def body(i, carry):
        keep = live[base + i] > 0
        block = blocks[listed[base + i]]
        out[i] = jnp.where(keep, block, jnp.zeros_like(block))
        return carry

    lax.fori_loop(0, per_step, body, 0)


def pick_blocks(blocks, listed, live):
    n = listed.shape[0]
    owned, height, rank = blocks.shape
    steps = 4
    per_step = n // steps
    return pl.pallas_call(
        functools.partial(pick_kernel, n, per_step),
        grid_spec=pltpu.PrefetchScalarGridSpec(
            num_scalar_prefetch=2,
            grid=(steps,),
            in_specs=[pl.BlockSpec((owned, height, rank), lambda s, *_: (0, 0, 0))],
            out_specs=pl.BlockSpec((per_step, height, rank), lambda s, *_: (s, 0, 0)),
        ),
        out_shape=jax.ShapeDtypeStruct((n, height, rank), BF16),
        compiler_params=pltpu.CompilerParams(vmem_limit_bytes=32 * MIB),
        name="pick_blocks",
    )(listed, live, blocks)


def weight_kernel(refs, values, out):
    n_blocks, users, height = out.shape
    slots = refs.shape[1]
    for u in range(users):
        ref = refs[u : u + 1, :]
        value = values[u : u + 1, :].astype(F32)
        block = ref // height
        row = ref % height
        hot_block = jnp.where(iota((n_blocks, slots), 0) == block, value, 0.0).astype(BF16)
        hot_row = jnp.where(iota((height, slots), 0) == row, 1.0, 0.0).astype(BF16)
        out[:, u, :] = lax.dot_general(hot_block, hot_row, (((1,), (1,)), ((), ())), preferred_element_type=F32)


def make_weights(refs, values, n_blocks, height):
    users, slots = refs.shape
    group = 8
    return pl.pallas_call(
        weight_kernel,
        grid=(users // group,),
        in_specs=[pl.BlockSpec((group, slots), lambda i: (i, 0))] * 2,
        out_specs=pl.BlockSpec((n_blocks, group, height), lambda i: (0, i, 0)),
        out_shape=jax.ShapeDtypeStruct((n_blocks, users, height), F32),
        compiler_params=pltpu.CompilerParams(vmem_limit_bytes=32 * MIB),
        name="make_weights",
    )(refs, values)


def gather_rows(wide, picked, refs, user):
    slots = picked.shape[0] // 2
    unroll = 16
    for base in range(0, slots, unroll):
        got = [wide[pl.ds(refs[user * slots + base + j], 2), :] for j in range(unroll)]
        for j in range(unroll):
            picked[2 * (base + j) : 2 * (base + j) + 2, :] = got[j]


def packed_terms(picked, value, store):
    slots = picked.shape[0] // 2
    low = picked[pl.ds(0, slots, stride=2), :].astype(BF16)
    high = picked[pl.ds(1, slots, stride=2), :].astype(BF16)
    mat = jnp.concatenate([low, high], axis=1)
    gram = dot_tn(mat, mat)
    linear = lax.dot_general(
        jnp.broadcast_to(value, (8, slots)), mat, (((1,), (0,)), ((), ())), preferred_element_type=F32
    )
    r, c = iota((128, 128), 0), iota((128, 128), 1)
    last = gram[128:, 128:]
    store(0, jnp.where(r >= c, gram[:128, :128], last))
    store(128, gram[:128, 128:])
    diag = jnp.sum(jnp.where(r == c, last, 0.0), axis=0, keepdims=True)
    row = iota((8, 128), 0)
    tail = jnp.where(row == 1, linear[:, :128], jnp.where(row == 2, linear[:, 128:], 0.0))
    store(256, jnp.where(row == 0, diag, tail))


def gram_kernel(
    refs, table, values, weights, out, gathered, wide, even, odd, stage, near, far, send_sem, recv_sem, give_sem, take_sem, own_sem
):
    rows = table.shape[0]
    share, height, _ = out.shape
    chunk, cut = 128, near.shape[2] // 16 * 8
    me, ring = lax.axis_index("grp"), 4
    after, before = (me + 1) % ring, (me + ring - 1) % ring
    u, peers = lax.axis_index("usr"), lax.axis_size("usr")
    cols = weights.shape[0] // peers

    barrier = pltpu.get_barrier_semaphore()
    for peer in (after, before):
        pl.semaphore_signal(barrier, inc=1, device_id={"grp": peer}, device_id_type=MESH)
    for o in range(1, peers):
        pl.semaphore_signal(barrier, inc=1, device_id={"usr": (u + o) % peers}, device_id_type=MESH)

    def give(o):
        peer = (u + o) % peers
        return pltpu.make_async_remote_copy(
            src_ref=weights.at[pl.ds(peer * cols, cols)],
            dst_ref=gathered.at[pl.ds(u * cols, cols)],
            send_sem=give_sem.at[o],
            recv_sem=take_sem.at[o],
            device_id={"usr": peer},
            device_id_type=MESH,
        )

    def take(o):
        peer = (u + peers - o) % peers
        slab = gathered.at[pl.ds(peer * cols, cols)]
        return pltpu.make_async_remote_copy(
            src_ref=slab,
            dst_ref=slab,
            send_sem=give_sem.at[o],
            recv_sem=take_sem.at[o],
            device_id={"usr": peer},
            device_id_type=MESH,
        )

    def widen(i, carry):
        part = table[pl.ds(i * chunk, chunk), :].astype(F32)
        wide[pl.ds(i * 2 * chunk, chunk, stride=2), :] = part[:, :128]
        wide[pl.ds(i * 2 * chunk + 1, chunk, stride=2), :] = part[:, 128:]
        return carry

    lax.fori_loop(0, rows // chunk, widen, 0)
    pl.semaphore_wait(barrier, peers + 1)

    keep = pltpu.make_async_copy(
        weights.at[pl.ds(u * cols, cols)], gathered.at[pl.ds(u * cols, cols)], own_sem
    )
    keep.start()

    def send_weights(o, carry):
        give(o).start()
        return carry

    lax.fori_loop(1, peers, send_weights, 0)

    def copy(j, kind):
        if kind == 0:
            src, dst, peer = stage.at[2, j, :cut], far.at[0, j, :cut], after
        elif kind == 1:
            src, dst, peer = stage.at[2, j, cut:], far.at[1, j, cut:], before
        elif kind == 2:
            src, dst, peer = stage.at[1, j], near.at[0, j], after
        else:
            src, dst, peer = stage.at[3, j], near.at[1, j], before
        return pltpu.make_async_remote_copy(
            src_ref=src,
            dst_ref=dst,
            send_sem=send_sem.at[j, kind],
            recv_sem=recv_sem.at[j, kind],
            device_id={"grp": peer},
            device_id_type=MESH,
        )

    def user(j, kind):
        return (me + kind) % ring * share + j

    def terms(picked, j, kind):
        def store(at, part):
            stage[kind, j, at : at + part.shape[0], :] = part

        packed_terms(picked, values[pl.ds(user(j, kind), 1), :].astype(BF16), store)

    def pass_on(j):
        copy(j, 0).wait_recv()
        stage[1, j, :cut, :] = stage[1, j, :cut, :] + far[0, j, :cut, :]
        copy(j, 2).start()
        copy(j, 1).wait_recv()
        stage[3, j, cut:, :] = stage[3, j, cut:, :] + far[1, j, cut:, :]
        copy(j, 3).start()

    def finish(j):
        copy(j, 2).wait_recv()
        copy(j, 3).wait_recv()
        out[j] = stage[0, j] + near[0, j] + near[1, j]

    gather_rows(wide, even, refs, user(0, 2))

    def furthest(i, carry):
        gather_rows(wide, odd, refs, user(2 * i + 1, 2))
        terms(even, 2 * i, 2)
        copy(2 * i, 0).start()
        copy(2 * i, 1).start()
        following = 2 * i + 2
        gather_rows(wide, even, refs, user(following % share, 2 - following // share))
        terms(odd, 2 * i + 1, 2)
        copy(2 * i + 1, 0).start()
        copy(2 * i + 1, 1).start()
        return carry

    lax.fori_loop(0, share // 2, furthest, 0)

    def neighbours(j, carry):
        gather_rows(wide, odd, refs, user(j, 3))
        terms(even, j, 1)
        following = j + 1
        gather_rows(wide, even, refs, user(following % share, 1 - following // share))
        terms(odd, j, 3)
        pass_on(j)
        return carry

    lax.fori_loop(0, share, neighbours, 0)

    def own_terms(i, carry):
        gather_rows(wide, odd, refs, user(2 * i + 1, 0))
        terms(even, 2 * i, 0)
        gather_rows(wide, even, refs, user((2 * i + 2) % share, 0))
        terms(odd, 2 * i + 1, 0)
        return carry

    lax.fori_loop(0, share // 2, own_terms, 0)

    def finish_all(j, carry):
        finish(j)
        return carry

    lax.fori_loop(0, share, finish_all, 0)

    def drain(j, carry):
        for kind in range(4):
            copy(j, kind).wait_send()
        return carry

    lax.fori_loop(0, share, drain, 0)

    def drain_weights(o, carry):
        give(o).wait_send()
        take(o).wait_recv()
        return carry

    lax.fori_loop(1, peers, drain_weights, 0)
    keep.wait()


def gram_terms(table, refs, values, weights):
    users, slots = refs.shape
    rows, rank = table.shape
    ring, height = 4, 264
    share = users // ring
    peers = lax.axis_size("usr")
    vmem = pl.BlockSpec(memory_space=pltpu.VMEM)
    hbm = pl.BlockSpec(memory_space=pltpu.HBM)
    return pl.pallas_call(
        gram_kernel,
        in_specs=[pl.BlockSpec(memory_space=pltpu.SMEM), vmem, vmem, hbm],
        out_specs=(vmem, hbm),
        out_shape=(
            jax.ShapeDtypeStruct((share, height, 128), F32),
            jax.ShapeDtypeStruct(weights.shape, F32),
        ),
        scratch_shapes=[
            pltpu.VMEM((2 * rows, 128), F32),
            pltpu.VMEM((2 * slots, 128), F32),
            pltpu.VMEM((2 * slots, 128), F32),
            pltpu.VMEM((ring, share, height, 128), F32),
            pltpu.VMEM((2, share, height, 128), F32),
            pltpu.VMEM((2, share, height, 128), F32),
            pltpu.SemaphoreType.DMA((share, 4)),
            pltpu.SemaphoreType.DMA((share, 4)),
            pltpu.SemaphoreType.DMA((peers,)),
            pltpu.SemaphoreType.DMA((peers,)),
            pltpu.SemaphoreType.DMA(()),
        ],
        compiler_params=pltpu.CompilerParams(vmem_limit_bytes=56 * MIB, collective_id=0, has_side_effects=True),
        cost_estimate=pl.CostEstimate(flops=60 * 10**9, bytes_accessed=200 * MIB, transcendentals=0),
        name="gram_terms",
    )((2 * refs).reshape(users * slots), table, values.astype(F32), weights)


def solve_kernel(packed, noise_cols, prior, shift, out, mats, right, back, sums):
    users = packed.shape[0]
    rank = prior.shape[0]
    half = rank // 2
    step = 32

    r, c = iota((half, half), 0), iota((half, half), 1)
    for m in range(users):
        both = packed[m, :half, :]
        cross = packed[m, half:rank, :]
        turned = both.T
        diag = packed[m, rank : rank + 1, :]
        first = jnp.where(r >= c, both, turned)
        last = jnp.where(r < c, both, jnp.where(r == c, diag, turned))
        mats[m, :half, :half] = prior[:half, :half] + ALPHA * first
        mats[m, :half, half:] = prior[:half, half:] + ALPHA * cross
        mats[m, half:, half:] = prior[half:, half:] + ALPHA * last
        right[m, 0:1, :half] = ALPHA * packed[m, rank + 1 : rank + 2, :] + shift[:, :half]
        right[m, 0:1, half:] = ALPHA * packed[m, rank + 2 : rank + 3, :] + shift[:, half:]

    sub = iota((1, 8, 128), 1)
    lane = iota((1, 8, 128), 2)
    tall_lane = iota((step, 128), 1)

    flat_lane = iota((8, 128), 1)

    def column(x, k):
        at = flat_lane // (2 * step) * (2 * step) + k
        return jnp.stack([jnp.take_along_axis(x[p], at, axis=1) for p in range(users // 2)])

    def later_work(m, k0, turn, rows, left, other):
        tile, group = k0 // half * half, k0 % half // step
        if not group:
            turn = pltpu.roll(turn, half - step, 1)
        keep = (tall_lane >= group * step) & (tall_lane < (group + 1) * step)
        turn = jnp.where(keep, turn, 0.0)
        back[m, k0 : k0 + step, :] = turn
        y = jnp.sum(turn * right[m, 0:1, tile : tile + half], axis=1, keepdims=True)
        right[m, 0:1, tile:] = right[m, 0:1, tile:] - jnp.sum(y * rows, axis=0, keepdims=True)
        sums[m, k0 : k0 + step, :] = jnp.broadcast_to(y + noise_cols[k0 : k0 + step, m : m + 1], (step, 128))
        low = k0 + 2 * step
        if low < rank:
            start = low // half * half
            change = dot_tn(left[:, start - tile :], other[:, start - tile :])
            mats[m, low:, start:] = mats[m, low:, start:] - change[low - start :]

    waiting = []
    for k0 in range(0, rank, step):
        tile, group = k0 // half * half, k0 % half // step
        parts, pivots = [], []
        for h in range(step // 8):
            rows = mats[:, k0 + 8 * h : k0 + 8 * h + 8, tile : tile + half]
            both = []
            for m in range(0, users, 2):
                turns = [(half - group * step) % half, (half + 2 * step - group * step) % half]
                one, two = [pltpu.roll(rows[m + e], turns[e], 1) if turns[e] else rows[m + e] for e in range(2)]
                both.append(jnp.where(lane[0] < 2 * step, one, two))
            unit = jnp.where(lane % step == sub + 8 * h, 1.0, 0.0)
            parts.append(jnp.where(lane % (2 * step) < step, jnp.stack(both), unit))
            pivots.append(jnp.ones((users // 2, 8, 128), F32))
        for k in range(0, step, 2):
            f, kk = k // 8, k % 8
            ones = [column(parts[h], k) for h in range(f, step // 8)]
            twos = [column(parts[h], k + 1) for h in range(f, step // 8)]
            a, b, c = ones[0][:, kk : kk + 1, :], twos[0][:, kk : kk + 1, :], twos[0][:, kk + 1 : kk + 2, :]
            low, high = parts[f][:, kk : kk + 1, :], parts[f][:, kk + 1 : kk + 2, :]
            inv = 1.0 / (a * c - b * b)
            ratio = b * (1.0 / a)
            first = (c * low - b * high) * inv
            second = (a * high - b * low) * inv
            second_row = parts[f] - ratio * low
            pivots[f] = jnp.where(sub == kk, a, jnp.where(sub == kk + 1, c - ratio * b, pivots[f]))
            for h in range(f, step // 8):
                new = parts[h] - ones[h - f] * first - twos[h - f] * second
                if h == f:
                    new = jnp.where(sub > kk + 1, new, jnp.where(sub == kk + 1, second_row, parts[h]))
                parts[h] = new
            if waiting:
                later_work(*waiting.pop(0))
        while waiting:
            later_work(*waiting.pop(0))
        scaled = [p * lax.rsqrt(v) for p, v in zip(parts, pivots)]
        for m in range(users):
            turn = jnp.concatenate([x[m // 2] for x in scaled], axis=0)
            at = (m % 2) * 2 * step + step
            turn = jnp.where((tall_lane >= at) & (tall_lane < at + step), turn, 0.0)
            ways = (step, 2 * step) if m % 2 == 0 else (2 * step, 3 * step)
            turn = turn + pltpu.roll(turn, ways[0], 1) + pltpu.roll(turn, ways[1], 1)
            hi, mid, low = split3(turn)
            one = jnp.where(tall_lane < step, 0.0, jnp.where(tall_lane < 3 * step, hi, mid))
            two = jnp.where(tall_lane < step, 0.0, jnp.where(tall_lane < 2 * step, hi, jnp.where(tall_lane < 3 * step, low, mid)))
            left = jnp.concatenate([one, two], axis=1).astype(BF16)
            hi, mid, low = split3(mats[m, k0 : k0 + step, tile:])
            other = jnp.concatenate([hi, hi, mid, hi, hi, low, hi, mid], axis=0).astype(BF16)
            rows = jnp.dot(left, other, preferred_element_type=F32)
            mats[m, k0 : k0 + step, tile:] = rows
            near = k0 + step
            left, other = stacked3(rows)
            if near < rank:
                start = near // half * half
                change = dot_tn(left[:, start - tile : start - tile + half], other[:, start - tile :])
                change = change[near - start : near - start + step]
                mats[m, near : near + step, start:] = mats[m, near : near + step, start:] - change
            waiting.append((m, k0, turn, rows, left, other))
    while waiting:
        later_work(*waiting.pop(0))

    x = [jnp.zeros((users, 1, half), F32)] * 2
    for k0 in range(rank - step, -1, -step):
        t = k0 // half
        at = pl.ds(k0, step)
        part = mats[:, at, half:] * x[1]
        if t == 0:
            part = part + mats[:, at, :half] * x[0]
        rest = sums[:, at, :] - jnp.sum(part, axis=2, keepdims=True)
        x[t] = x[t] + jnp.sum(back[:, at, :] * rest, axis=1, keepdims=True)
    for m in range(users):
        out[m : m + 1, :half] = x[0][m]
        out[m : m + 1, half:] = x[1][m]


def solve_users(packed, noise, prior, shift):
    users = packed.shape[0]
    rank = prior.shape[0]
    vmem = pl.BlockSpec(memory_space=pltpu.VMEM)
    return pl.pallas_call(
        solve_kernel,
        in_specs=[vmem] * 4,
        out_specs=vmem,
        out_shape=jax.ShapeDtypeStruct((users, rank), F32),
        scratch_shapes=[
            pltpu.VMEM((users, rank, rank), F32),
            pltpu.VMEM((users, 8, rank), F32),
            pltpu.VMEM((users, rank, 128), F32),
            pltpu.VMEM((users, rank, 128), F32),
        ],
        compiler_params=pltpu.CompilerParams(vmem_limit_bytes=48 * MIB),
        name="solve_users",
    )(packed, noise.T, prior, shift.reshape(1, rank))


def share_kernel(own, out, first_send, first_recv, x_send, x_recv, z_send, z_recv, twin_send, twin_recv):
    g, u = lax.axis_index("grp"), lax.axis_index("usr")
    ring, side = 4, 4
    core, x, z = u % 2, u // 2 % side, u // (2 * side)
    twin = u + 1 - 2 * core
    cut = ring // 2

    def place(dz, dx):
        return (z + dz + side) % side * (2 * side) + (x + dx + side) % side * 2 + core

    barrier = pltpu.get_barrier_semaphore()
    for o in range(1, ring):
        pl.semaphore_signal(barrier, inc=1, device_id={"grp": (g + o) % ring}, device_id_type=MESH)
    for peer in (place(0, 1), place(0, -1), place(1, 0), place(-1, 0), twin):
        pl.semaphore_signal(barrier, inc=1, device_id={"usr": peer}, device_id_type=MESH)
    pl.semaphore_wait(barrier, ring - 1 + 5)

    started = []

    def remote(src, dst, send, recv, peer):
        return pltpu.make_async_remote_copy(
            src_ref=src, dst_ref=dst, send_sem=send, recv_sem=recv, device_id=peer, device_id_type=MESH
        )

    def send(slab, sems, k, peer):
        c = remote(slab, slab, sems[0].at[k], sems[1].at[k], {"usr": peer})
        c.start()
        started.append(c)

    def wait(slab, sems, k):
        remote(slab, slab, sems[0].at[k], sems[1].at[k], {"usr": twin}).wait_recv()

    x_sems, z_sems, twin_sems = (x_send, x_recv), (z_send, z_recv), (twin_send, twin_recv)
    twins = []

    def to_twin(dz, dx):
        k = len(twins)
        twins.append(k)
        send(out.at[place(dz, dx)], twin_sems, k, twin)

    for o in range(1, ring):
        c = remote(own, out.at[u, g], first_send.at[o - 1], first_recv.at[o - 1], {"grp": (g + o) % ring})
        c.start()
        started.append(c)
    out[u, g] = own[...]
    for o in range(1, ring):
        src = (g + ring - o) % ring
        remote(own, out.at[u, src], first_send.at[o - 1], first_recv.at[o - 1], {"grp": src}).wait_recv()

    columns = (0, -1, 1, 2)

    def along_z(i):
        slab = out.at[place(0, columns[i])]
        send(slab, z_sems, 4 * i, place(1, 0))
        send(slab, z_sems, 4 * i + 1, place(-1, 0))

    send(out.at[u], x_sems, 0, place(0, 1))
    send(out.at[u], x_sems, 1, place(0, -1))
    along_z(0)
    to_twin(0, 0)
    wait(out.at[place(0, -1)], x_sems, 0)
    send(out.at[place(0, -1), :cut], x_sems, 2, place(0, 1))
    along_z(1)
    wait(out.at[place(0, 1)], x_sems, 1)
    send(out.at[place(0, 1), cut:], x_sems, 3, place(0, -1))
    along_z(2)
    to_twin(0, -1)
    to_twin(0, 1)
    wait(out.at[place(0, 2), :cut], x_sems, 2)
    wait(out.at[place(0, 2), cut:], x_sems, 3)
    along_z(3)
    to_twin(0, 2)
    for i, dx in enumerate(columns):
        wait(out.at[place(-1, dx)], z_sems, 4 * i)
        send(out.at[place(-1, dx), :cut], z_sems, 4 * i + 2, place(1, 0))
        wait(out.at[place(1, dx)], z_sems, 4 * i + 1)
        send(out.at[place(1, dx), cut:], z_sems, 4 * i + 3, place(-1, 0))
        to_twin(-1, dx)
        to_twin(1, dx)
    for i, dx in enumerate(columns):
        wait(out.at[place(2, dx), :cut], z_sems, 4 * i + 2)
        wait(out.at[place(2, dx), cut:], z_sems, 4 * i + 3)
        to_twin(2, dx)
    for k in twins:
        wait(out.at[u], twin_sems, k)
    for c in started:
        c.wait_send()


def share_samples(own):
    share, rank = own.shape
    peers, ring = lax.axis_size("usr"), lax.axis_size("grp")
    vmem = pl.BlockSpec(memory_space=pltpu.VMEM)
    dma = pltpu.SemaphoreType.DMA
    return pl.pallas_call(
        share_kernel,
        in_specs=[vmem],
        out_specs=vmem,
        out_shape=jax.ShapeDtypeStruct((peers, ring, share, rank), F32),
        scratch_shapes=[dma((n,)) for n in (3, 3, 4, 4, 16, 16, 16, 16)],
        compiler_params=pltpu.CompilerParams(vmem_limit_bytes=32 * MIB, collective_id=1, has_side_effects=True),
        name="share_samples",
    )(own)


def stats_kernel(cols, listed, live, weights, samples, out, held):
    out[...] = jnp.zeros_like(out)
    parts, share = samples.shape[1:3]
    unroll = 4

    def device(d):
        for g in range(parts):
            held[g * share : (g + 1) * share, :] = samples[d, g]
        hi, lo = split(held[...])
        other = jnp.concatenate([hi, lo, hi], axis=0).astype(BF16)
        terms = []
        for c in range(cols):
            hi, lo = split(jnp.where(live[d * cols + c] > 0, ALPHA * weights[d * cols + c], 0.0))
            left = jnp.concatenate([hi, hi, lo], axis=0).astype(BF16)
            terms.append(dot_tn(left, other))
        for c in range(cols):
            b = listed[d * cols + c]
            out[b] = out[b] + terms[c]

    def devices(i, carry):
        for e in range(unroll):
            device(unroll * i + e)
        return carry

    lax.fori_loop(0, samples.shape[0] // unroll, devices, 0)


def make_stats(weights, samples, listed, live, owned):
    n, users, height = weights.shape
    peers, _, _, rank = samples.shape
    vmem = pl.BlockSpec(memory_space=pltpu.VMEM)
    smem = pl.BlockSpec(memory_space=pltpu.SMEM)
    return pl.pallas_call(
        functools.partial(stats_kernel, n // peers),
        in_specs=[smem, smem, vmem, vmem],
        out_specs=vmem,
        out_shape=jax.ShapeDtypeStruct((owned, height, rank), F32),
        scratch_shapes=[pltpu.VMEM((users, rank), F32)],
        compiler_params=pltpu.CompilerParams(vmem_limit_bytes=32 * MIB),
        name="make_stats",
    )(listed, live, weights, samples)


def on_device(item_factors, send_ids, send_count, rating_pointer, rating_value, noise, prior_prec, prior_shift):
    peers = lax.axis_size("usr")
    blocks = item_factors[0]
    owned, height, rank = blocks.shape
    cols = send_ids.shape[-1]
    n = peers * cols
    listed = send_ids[0, 0].reshape(n)
    live = (jnp.arange(cols, dtype=jnp.int32)[None, :] < send_count[0, 0][:, None]).astype(jnp.int32).reshape(n)
    refs, values = rating_pointer[0], rating_value[0]

    outgoing = pick_blocks(blocks, listed, live)
    incoming = lax.all_to_all(outgoing, "usr", split_axis=0, concat_axis=0, tiled=True)
    weights = make_weights(refs, values, n, height)
    packed, gathered = gram_terms(incoming.reshape(n * height, rank), refs, values, weights)
    share = packed.shape[0]
    draws = lax.dynamic_slice_in_dim(noise, lax.axis_index("grp") * share, share, 0)
    everyone = share_samples(solve_users(packed, draws, prior_prec, prior_shift))
    samples = lax.dynamic_index_in_dim(everyone, lax.axis_index("usr"), 0, keepdims=False)
    samples = samples.reshape(refs.shape[0], rank)
    stats = make_stats(gathered, everyone, listed, live, owned)
    return (samples, stats[None])


def solution(mesh):
    placed = (
        P("grp", "usr", None, None),
        P("grp", "usr", None, None),
        P("grp", "usr", None),
        P("grp", "usr", None),
        P("grp", "usr", None),
        P("usr", None),
        P(),
        P(),
    )
    return jax.shard_map(
        on_device,
        mesh=mesh,
        in_specs=placed,
        out_specs=(P("usr", None), P("grp", "usr", None, None)),
        check_vma=False,
    )
```

```python
import functools

import jax
import jax.numpy as jnp
from jax import lax
from jax.experimental import pallas as pl
from jax.experimental.pallas import tpu as pltpu
from jax.sharding import PartitionSpec as P

ALPHA = 2.0
F32 = jnp.float32
BF16 = jnp.bfloat16
MIB = 2**20
MESH = pl.DeviceIdType.MESH


def iota(shape, dim):
    return lax.broadcasted_iota(jnp.int32, shape, dim)


def split(x):
    hi = x.astype(BF16).astype(F32)
    return hi, x - hi


def split3(x):
    hi = x.astype(BF16).astype(F32)
    rest = x - hi
    mid = rest.astype(BF16).astype(F32)
    return hi, mid, rest - mid


def stacked3(x):
    hi, mid, low = split3(x)
    left = jnp.concatenate([hi, hi, mid, hi, low, mid], axis=0).astype(BF16)
    right = jnp.concatenate([hi, mid, hi, low, hi, mid], axis=0).astype(BF16)
    return left, right


def dot_tn(a, b):
    return lax.dot_general(a, b, (((0,), (0,)), ((), ())), preferred_element_type=F32)


def pick_kernel(cols, per_step, listed, live, blocks, out):
    base = pl.program_id(0) * per_step

    def body(i, carry):
        keep = live[base + i] > 0
        block = blocks[listed[base + i]]
        out[i] = jnp.where(keep, block, jnp.zeros_like(block))
        return carry

    lax.fori_loop(0, per_step, body, 0)


def pick_blocks(blocks, listed, live):
    n = listed.shape[0]
    owned, height, rank = blocks.shape
    steps = 4
    per_step = n // steps
    return pl.pallas_call(
        functools.partial(pick_kernel, n, per_step),
        grid_spec=pltpu.PrefetchScalarGridSpec(
            num_scalar_prefetch=2,
            grid=(steps,),
            in_specs=[pl.BlockSpec((owned, height, rank), lambda s, *_: (0, 0, 0))],
            out_specs=pl.BlockSpec((per_step, height, rank), lambda s, *_: (s, 0, 0)),
        ),
        out_shape=jax.ShapeDtypeStruct((n, height, rank), BF16),
        compiler_params=pltpu.CompilerParams(vmem_limit_bytes=32 * MIB),
        name="pick_blocks",
    )(listed, live, blocks)


def weight_kernel(refs, values, out):
    n_blocks, users, height = out.shape
    slots = refs.shape[1]
    for u in range(users):
        ref = refs[u : u + 1, :]
        value = values[u : u + 1, :].astype(F32)
        block = ref // height
        row = ref % height
        hot_block = jnp.where(iota((n_blocks, slots), 0) == block, value, 0.0).astype(BF16)
        hot_row = jnp.where(iota((height, slots), 0) == row, 1.0, 0.0).astype(BF16)
        out[:, u, :] = lax.dot_general(hot_block, hot_row, (((1,), (1,)), ((), ())), preferred_element_type=F32)


def make_weights(refs, values, n_blocks, height):
    users, slots = refs.shape
    group = 8
    return pl.pallas_call(
        weight_kernel,
        grid=(users // group,),
        in_specs=[pl.BlockSpec((group, slots), lambda i: (i, 0))] * 2,
        out_specs=pl.BlockSpec((n_blocks, group, height), lambda i: (0, i, 0)),
        out_shape=jax.ShapeDtypeStruct((n_blocks, users, height), F32),
        compiler_params=pltpu.CompilerParams(vmem_limit_bytes=32 * MIB),
        name="make_weights",
    )(refs, values)


def gather_rows(wide, picked, refs, user):
    slots = picked.shape[0] // 2
    unroll = 16
    for base in range(0, slots, unroll):
        got = [wide[pl.ds(refs[user * slots + base + j], 2), :] for j in range(unroll)]
        for j in range(unroll):
            picked[2 * (base + j) : 2 * (base + j) + 2, :] = got[j]


def packed_terms(picked, value, store):
    slots = picked.shape[0] // 2
    low = picked[pl.ds(0, slots, stride=2), :].astype(BF16)
    high = picked[pl.ds(1, slots, stride=2), :].astype(BF16)
    mat = jnp.concatenate([low, high], axis=1)
    gram = dot_tn(mat, mat)
    linear = lax.dot_general(
        jnp.broadcast_to(value, (8, slots)), mat, (((1,), (0,)), ((), ())), preferred_element_type=F32
    )
    r, c = iota((128, 128), 0), iota((128, 128), 1)
    last = gram[128:, 128:]
    store(0, jnp.where(r >= c, gram[:128, :128], last))
    store(128, gram[:128, 128:])
    diag = jnp.sum(jnp.where(r == c, last, 0.0), axis=0, keepdims=True)
    row = iota((8, 128), 0)
    tail = jnp.where(row == 1, linear[:, :128], jnp.where(row == 2, linear[:, 128:], 0.0))
    store(256, jnp.where(row == 0, diag, tail))


def gram_kernel(
    refs, table, values, weights, out, gathered, wide, even, odd, stage, near, far, send_sem, recv_sem, give_sem, take_sem, own_sem
):
    rows = table.shape[0]
    share, height, _ = out.shape
    chunk, cut = 128, near.shape[2] // 16 * 8
    me, ring = lax.axis_index("grp"), 4
    after, before = (me + 1) % ring, (me + ring - 1) % ring
    u, peers = lax.axis_index("usr"), lax.axis_size("usr")
    cols = weights.shape[0] // peers

    barrier = pltpu.get_barrier_semaphore()
    for peer in (after, before):
        pl.semaphore_signal(barrier, inc=1, device_id={"grp": peer}, device_id_type=MESH)
    for o in range(1, peers):
        pl.semaphore_signal(barrier, inc=1, device_id={"usr": (u + o) % peers}, device_id_type=MESH)

    def give(o):
        peer = (u + o) % peers
        return pltpu.make_async_remote_copy(
            src_ref=weights.at[pl.ds(peer * cols, cols)],
            dst_ref=gathered.at[pl.ds(u * cols, cols)],
            send_sem=give_sem.at[o],
            recv_sem=take_sem.at[o],
            device_id={"usr": peer},
            device_id_type=MESH,
        )

    def take(o):
        peer = (u + peers - o) % peers
        slab = gathered.at[pl.ds(peer * cols, cols)]
        return pltpu.make_async_remote_copy(
            src_ref=slab,
            dst_ref=slab,
            send_sem=give_sem.at[o],
            recv_sem=take_sem.at[o],
            device_id={"usr": peer},
            device_id_type=MESH,
        )

    def widen(i, carry):
        part = table[pl.ds(i * chunk, chunk), :].astype(F32)
        wide[pl.ds(i * 2 * chunk, chunk, stride=2), :] = part[:, :128]
        wide[pl.ds(i * 2 * chunk + 1, chunk, stride=2), :] = part[:, 128:]
        return carry

    lax.fori_loop(0, rows // chunk, widen, 0, unroll=4)
    pl.semaphore_wait(barrier, peers + 1)

    keep = pltpu.make_async_copy(
        weights.at[pl.ds(u * cols, cols)], gathered.at[pl.ds(u * cols, cols)], own_sem
    )
    keep.start()

    def send_weights(o, carry):
        give(o).start()
        return carry

    lax.fori_loop(1, peers, send_weights, 0)

    def copy(j, kind):
        if kind == 0:
            src, dst, peer = stage.at[2, j, :cut], far.at[0, j, :cut], after
        elif kind == 1:
            src, dst, peer = stage.at[2, j, cut:], far.at[1, j, cut:], before
        elif kind == 2:
            src, dst, peer = stage.at[1, j], near.at[0, j], after
        else:
            src, dst, peer = stage.at[3, j], near.at[1, j], before
        return pltpu.make_async_remote_copy(
            src_ref=src,
            dst_ref=dst,
            send_sem=send_sem.at[j, kind],
            recv_sem=recv_sem.at[j, kind],
            device_id={"grp": peer},
            device_id_type=MESH,
        )

    def user(j, kind):
        return (me + kind) % ring * share + j

    def terms(picked, j, kind):
        def store(at, part):
            stage[kind, j, at : at + part.shape[0], :] = part

        packed_terms(picked, values[pl.ds(user(j, kind), 1), :].astype(BF16), store)

    def pass_on(j):
        copy(j, 0).wait_recv()
        stage[1, j, :cut, :] = stage[1, j, :cut, :] + far[0, j, :cut, :]
        copy(j, 2).start()
        copy(j, 1).wait_recv()
        stage[3, j, cut:, :] = stage[3, j, cut:, :] + far[1, j, cut:, :]
        copy(j, 3).start()

    def finish(j):
        copy(j, 2).wait_recv()
        copy(j, 3).wait_recv()
        out[j] = stage[0, j] + near[0, j] + near[1, j]

    gather_rows(wide, even, refs, user(0, 2))

    def furthest(i, carry):
        gather_rows(wide, odd, refs, user(2 * i + 1, 2))
        terms(even, 2 * i, 2)
        copy(2 * i, 0).start()
        copy(2 * i, 1).start()
        following = 2 * i + 2
        gather_rows(wide, even, refs, user(following % share, 2 - following // share))
        terms(odd, 2 * i + 1, 2)
        copy(2 * i + 1, 0).start()
        copy(2 * i + 1, 1).start()
        return carry

    lax.fori_loop(0, share // 2, furthest, 0)

    def neighbours(j, carry):
        gather_rows(wide, odd, refs, user(j, 3))
        terms(even, j, 1)
        following = j + 1
        gather_rows(wide, even, refs, user(following % share, 1 - following // share))
        terms(odd, j, 3)
        pass_on(j)
        return carry

    lax.fori_loop(0, share, neighbours, 0)

    def own_terms(i, carry):
        gather_rows(wide, odd, refs, user(2 * i + 1, 0))
        terms(even, 2 * i, 0)
        gather_rows(wide, even, refs, user((2 * i + 2) % share, 0))
        terms(odd, 2 * i + 1, 0)
        return carry

    lax.fori_loop(0, share // 2, own_terms, 0)

    def finish_all(j, carry):
        finish(j)
        return carry

    lax.fori_loop(0, share, finish_all, 0)

    def drain(j, carry):
        for kind in range(4):
            copy(j, kind).wait_send()
        return carry

    lax.fori_loop(0, share, drain, 0)

    def drain_weights(o, carry):
        give(o).wait_send()
        take(o).wait_recv()
        return carry

    lax.fori_loop(1, peers, drain_weights, 0)
    keep.wait()


def gram_terms(table, refs, values, weights):
    users, slots = refs.shape
    rows, rank = table.shape
    ring, height = 4, 264
    share = users // ring
    peers = lax.axis_size("usr")
    vmem = pl.BlockSpec(memory_space=pltpu.VMEM)
    hbm = pl.BlockSpec(memory_space=pltpu.HBM)
    return pl.pallas_call(
        gram_kernel,
        in_specs=[pl.BlockSpec(memory_space=pltpu.SMEM), vmem, vmem, hbm],
        out_specs=(vmem, hbm),
        out_shape=(
            jax.ShapeDtypeStruct((share, height, 128), F32),
            jax.ShapeDtypeStruct(weights.shape, F32),
        ),
        scratch_shapes=[
            pltpu.VMEM((2 * rows, 128), F32),
            pltpu.VMEM((2 * slots, 128), F32),
            pltpu.VMEM((2 * slots, 128), F32),
            pltpu.VMEM((ring, share, height, 128), F32),
            pltpu.VMEM((2, share, height, 128), F32),
            pltpu.VMEM((2, share, height, 128), F32),
            pltpu.SemaphoreType.DMA((share, 4)),
            pltpu.SemaphoreType.DMA((share, 4)),
            pltpu.SemaphoreType.DMA((peers,)),
            pltpu.SemaphoreType.DMA((peers,)),
            pltpu.SemaphoreType.DMA(()),
        ],
        compiler_params=pltpu.CompilerParams(vmem_limit_bytes=56 * MIB, collective_id=0, has_side_effects=True),
        cost_estimate=pl.CostEstimate(flops=60 * 10**9, bytes_accessed=200 * MIB, transcendentals=0),
        name="gram_terms",
    )((2 * refs).reshape(users * slots), table, values.astype(F32), weights)


def solve_kernel(packed, noise_cols, prior, shift, out, mats, right, back, sums):
    users = packed.shape[0]
    rank = prior.shape[0]
    half = rank // 2
    step = 32

    r, c = iota((half, half), 0), iota((half, half), 1)
    for m in range(users):
        both = packed[m, :half, :]
        cross = packed[m, half:rank, :]
        turned = both.T
        diag = packed[m, rank : rank + 1, :]
        first = jnp.where(r >= c, both, turned)
        last = jnp.where(r < c, both, jnp.where(r == c, diag, turned))
        mats[m, :half, :half] = prior[:half, :half] + ALPHA * first
        mats[m, :half, half:] = prior[:half, half:] + ALPHA * cross
        mats[m, half:, half:] = prior[half:, half:] + ALPHA * last
        right[m, 0:1, :half] = ALPHA * packed[m, rank + 1 : rank + 2, :] + shift[:, :half]
        right[m, 0:1, half:] = ALPHA * packed[m, rank + 2 : rank + 3, :] + shift[:, half:]

    sub = iota((1, 8, 128), 1)
    lane = iota((1, 8, 128), 2)
    tall_lane = iota((step, 128), 1)

    flat_lane = iota((8, 128), 1)

    def column(x, k):
        at = flat_lane // (2 * step) * (2 * step) + k
        return jnp.stack([jnp.take_along_axis(x[p], at, axis=1) for p in range(users // 2)])

    def later_work(m, k0, turn, rows, left, other):
        tile, group = k0 // half * half, k0 % half // step
        if not group:
            turn = pltpu.roll(turn, half - step, 1)
        keep = (tall_lane >= group * step) & (tall_lane < (group + 1) * step)
        turn = jnp.where(keep, turn, 0.0)
        back[m, k0 : k0 + step, :] = turn
        y = jnp.sum(turn * right[m, 0:1, tile : tile + half], axis=1, keepdims=True)
        right[m, 0:1, tile:] = right[m, 0:1, tile:] - jnp.sum(y * rows, axis=0, keepdims=True)
        sums[m, k0 : k0 + step, :] = jnp.broadcast_to(y + noise_cols[k0 : k0 + step, m : m + 1], (step, 128))
        low = k0 + 2 * step
        if low < rank:
            start = low // half * half
            change = dot_tn(left[:, start - tile :], other[:, start - tile :])
            mats[m, low:, start:] = mats[m, low:, start:] - change[low - start :]

    waiting = []
    for k0 in range(0, rank, step):
        tile, group = k0 // half * half, k0 % half // step
        parts, pivots = [], []
        for h in range(step // 8):
            rows = mats[:, k0 + 8 * h : k0 + 8 * h + 8, tile : tile + half]
            both = []
            for m in range(0, users, 2):
                turns = [(half - group * step) % half, (half + 2 * step - group * step) % half]
                one, two = [pltpu.roll(rows[m + e], turns[e], 1) if turns[e] else rows[m + e] for e in range(2)]
                both.append(jnp.where(lane[0] < 2 * step, one, two))
            unit = jnp.where(lane % step == sub + 8 * h, 1.0, 0.0)
            parts.append(jnp.where(lane % (2 * step) < step, jnp.stack(both), unit))
            pivots.append(jnp.ones((users // 2, 8, 128), F32))
        for k in range(0, step, 2):
            f, kk = k // 8, k % 8
            ones = [column(parts[h], k) for h in range(f, step // 8)]
            twos = [column(parts[h], k + 1) for h in range(f, step // 8)]
            a, b, c = ones[0][:, kk : kk + 1, :], twos[0][:, kk : kk + 1, :], twos[0][:, kk + 1 : kk + 2, :]
            low, high = parts[f][:, kk : kk + 1, :], parts[f][:, kk + 1 : kk + 2, :]
            inv = 1.0 / (a * c - b * b)
            ratio = b * (1.0 / a)
            first = (c * low - b * high) * inv
            second = (a * high - b * low) * inv
            second_row = parts[f] - ratio * low
            pivots[f] = jnp.where(sub == kk, a, jnp.where(sub == kk + 1, c - ratio * b, pivots[f]))
            for h in range(f, step // 8):
                new = parts[h] - ones[h - f] * first - twos[h - f] * second
                if h == f:
                    new = jnp.where(sub > kk + 1, new, jnp.where(sub == kk + 1, second_row, parts[h]))
                parts[h] = new
            if waiting:
                later_work(*waiting.pop(0))
        while waiting:
            later_work(*waiting.pop(0))
        scaled = [p * lax.rsqrt(v) for p, v in zip(parts, pivots)]
        for m in range(users):
            turn = jnp.concatenate([x[m // 2] for x in scaled], axis=0)
            at = (m % 2) * 2 * step + step
            turn = jnp.where((tall_lane >= at) & (tall_lane < at + step), turn, 0.0)
            ways = (step, 2 * step) if m % 2 == 0 else (2 * step, 3 * step)
            turn = turn + pltpu.roll(turn, ways[0], 1) + pltpu.roll(turn, ways[1], 1)
            hi, mid, low = split3(turn)
            one = jnp.where(tall_lane < step, 0.0, jnp.where(tall_lane < 3 * step, hi, mid))
            two = jnp.where(tall_lane < step, 0.0, jnp.where(tall_lane < 2 * step, hi, jnp.where(tall_lane < 3 * step, low, mid)))
            left = jnp.concatenate([one, two], axis=1).astype(BF16)
            hi, mid, low = split3(mats[m, k0 : k0 + step, tile:])
            other = jnp.concatenate([hi, hi, mid, hi, hi, low, hi, mid], axis=0).astype(BF16)
            rows = jnp.dot(left, other, preferred_element_type=F32)
            mats[m, k0 : k0 + step, tile:] = rows
            near = k0 + step
            left, other = stacked3(rows)
            if near < rank:
                start = near // half * half
                change = dot_tn(left[:, start - tile : start - tile + half], other[:, start - tile :])
                change = change[near - start : near - start + step]
                mats[m, near : near + step, start:] = mats[m, near : near + step, start:] - change
            waiting.append((m, k0, turn, rows, left, other))
    while waiting:
        later_work(*waiting.pop(0))

    x = [jnp.zeros((users, 1, half), F32)] * 2
    for k0 in range(rank - step, -1, -step):
        t = k0 // half
        at = pl.ds(k0, step)
        part = mats[:, at, half:] * x[1]
        if t == 0:
            part = part + mats[:, at, :half] * x[0]
        rest = sums[:, at, :] - jnp.sum(part, axis=2, keepdims=True)
        x[t] = x[t] + jnp.sum(back[:, at, :] * rest, axis=1, keepdims=True)
    for m in range(users):
        out[m : m + 1, :half] = x[0][m]
        out[m : m + 1, half:] = x[1][m]


def solve_users(packed, noise, prior, shift):
    users = packed.shape[0]
    rank = prior.shape[0]
    vmem = pl.BlockSpec(memory_space=pltpu.VMEM)
    return pl.pallas_call(
        solve_kernel,
        in_specs=[vmem] * 4,
        out_specs=vmem,
        out_shape=jax.ShapeDtypeStruct((users, rank), F32),
        scratch_shapes=[
            pltpu.VMEM((users, rank, rank), F32),
            pltpu.VMEM((users, 8, rank), F32),
            pltpu.VMEM((users, rank, 128), F32),
            pltpu.VMEM((users, rank, 128), F32),
        ],
        compiler_params=pltpu.CompilerParams(vmem_limit_bytes=48 * MIB),
        name="solve_users",
    )(packed, noise.T, prior, shift.reshape(1, rank))


def share_kernel(own, out, first_send, first_recv, x_send, x_recv, z_send, z_recv, twin_send, twin_recv):
    g, u = lax.axis_index("grp"), lax.axis_index("usr")
    ring, side = 4, 4
    core, x, z = u % 2, u // 2 % side, u // (2 * side)
    twin = u + 1 - 2 * core
    cut = ring // 2

    def place(dz, dx):
        return (z + dz + side) % side * (2 * side) + (x + dx + side) % side * 2 + core

    barrier = pltpu.get_barrier_semaphore()
    for o in range(1, ring):
        pl.semaphore_signal(barrier, inc=1, device_id={"grp": (g + o) % ring}, device_id_type=MESH)
    for peer in (place(0, 1), place(0, -1), place(1, 0), place(-1, 0), twin):
        pl.semaphore_signal(barrier, inc=1, device_id={"usr": peer}, device_id_type=MESH)
    pl.semaphore_wait(barrier, ring - 1 + 5)

    started = []

    def remote(src, dst, send, recv, peer):
        return pltpu.make_async_remote_copy(
            src_ref=src, dst_ref=dst, send_sem=send, recv_sem=recv, device_id=peer, device_id_type=MESH
        )

    def send(slab, sems, k, peer):
        c = remote(slab, slab, sems[0].at[k], sems[1].at[k], {"usr": peer})
        c.start()
        started.append(c)

    def wait(slab, sems, k):
        remote(slab, slab, sems[0].at[k], sems[1].at[k], {"usr": twin}).wait_recv()

    x_sems, z_sems, twin_sems = (x_send, x_recv), (z_send, z_recv), (twin_send, twin_recv)
    twins = []

    def to_twin(dz, dx):
        k = len(twins)
        twins.append(k)
        send(out.at[place(dz, dx)], twin_sems, k, twin)

    for o in range(1, ring):
        c = remote(own, out.at[u, g], first_send.at[o - 1], first_recv.at[o - 1], {"grp": (g + o) % ring})
        c.start()
        started.append(c)
    out[u, g] = own[...]
    for o in range(1, ring):
        src = (g + ring - o) % ring
        remote(own, out.at[u, src], first_send.at[o - 1], first_recv.at[o - 1], {"grp": src}).wait_recv()

    columns = (0, -1, 1, 2)

    def along_z(i):
        slab = out.at[place(0, columns[i])]
        send(slab, z_sems, 4 * i, place(1, 0))
        send(slab, z_sems, 4 * i + 1, place(-1, 0))

    send(out.at[u], x_sems, 0, place(0, 1))
    send(out.at[u], x_sems, 1, place(0, -1))
    along_z(0)
    to_twin(0, 0)
    wait(out.at[place(0, -1)], x_sems, 0)
    send(out.at[place(0, -1), :cut], x_sems, 2, place(0, 1))
    along_z(1)
    wait(out.at[place(0, 1)], x_sems, 1)
    send(out.at[place(0, 1), cut:], x_sems, 3, place(0, -1))
    along_z(2)
    to_twin(0, -1)
    to_twin(0, 1)
    wait(out.at[place(0, 2), :cut], x_sems, 2)
    wait(out.at[place(0, 2), cut:], x_sems, 3)
    along_z(3)
    to_twin(0, 2)
    for i, dx in enumerate(columns):
        wait(out.at[place(-1, dx)], z_sems, 4 * i)
        send(out.at[place(-1, dx), :cut], z_sems, 4 * i + 2, place(1, 0))
        wait(out.at[place(1, dx)], z_sems, 4 * i + 1)
        send(out.at[place(1, dx), cut:], z_sems, 4 * i + 3, place(-1, 0))
        to_twin(-1, dx)
        to_twin(1, dx)
    for i, dx in enumerate(columns):
        wait(out.at[place(2, dx), :cut], z_sems, 4 * i + 2)
        wait(out.at[place(2, dx), cut:], z_sems, 4 * i + 3)
        to_twin(2, dx)
    for k in twins:
        wait(out.at[u], twin_sems, k)
    for c in started:
        c.wait_send()


def share_samples(own):
    share, rank = own.shape
    peers, ring = lax.axis_size("usr"), lax.axis_size("grp")
    vmem = pl.BlockSpec(memory_space=pltpu.VMEM)
    dma = pltpu.SemaphoreType.DMA
    return pl.pallas_call(
        share_kernel,
        in_specs=[vmem],
        out_specs=vmem,
        out_shape=jax.ShapeDtypeStruct((peers, ring, share, rank), F32),
        scratch_shapes=[dma((n,)) for n in (3, 3, 4, 4, 16, 16, 16, 16)],
        compiler_params=pltpu.CompilerParams(vmem_limit_bytes=32 * MIB, collective_id=1, has_side_effects=True),
        name="share_samples",
    )(own)


def stats_kernel(cols, listed, live, weights, samples, out, held):
    out[...] = jnp.zeros_like(out)
    parts, share = samples.shape[1:3]
    unroll = 4

    def device(d):
        for g in range(parts):
            held[g * share : (g + 1) * share, :] = samples[d, g]
        hi, lo = split(held[...])
        other = jnp.concatenate([hi, lo, hi], axis=0).astype(BF16)
        terms = []
        for c in range(cols):
            hi, lo = split(jnp.where(live[d * cols + c] > 0, ALPHA * weights[d * cols + c], 0.0))
            left = jnp.concatenate([hi, hi, lo], axis=0).astype(BF16)
            terms.append(dot_tn(left, other))
        for c in range(cols):
            b = listed[d * cols + c]
            out[b] = out[b] + terms[c]

    def devices(i, carry):
        for e in range(unroll):
            device(unroll * i + e)
        return carry

    lax.fori_loop(0, samples.shape[0] // unroll, devices, 0)


def make_stats(weights, samples, listed, live, owned):
    n, users, height = weights.shape
    peers, _, _, rank = samples.shape
    vmem = pl.BlockSpec(memory_space=pltpu.VMEM)
    smem = pl.BlockSpec(memory_space=pltpu.SMEM)
    return pl.pallas_call(
        functools.partial(stats_kernel, n // peers),
        in_specs=[smem, smem, vmem, vmem],
        out_specs=vmem,
        out_shape=jax.ShapeDtypeStruct((owned, height, rank), F32),
        scratch_shapes=[pltpu.VMEM((users, rank), F32)],
        compiler_params=pltpu.CompilerParams(vmem_limit_bytes=32 * MIB),
        name="make_stats",
    )(listed, live, weights, samples)


def on_device(item_factors, send_ids, send_count, rating_pointer, rating_value, noise, prior_prec, prior_shift):
    peers = lax.axis_size("usr")
    blocks = item_factors[0]
    owned, height, rank = blocks.shape
    cols = send_ids.shape[-1]
    n = peers * cols
    listed = send_ids[0, 0].reshape(n)
    live = (jnp.arange(cols, dtype=jnp.int32)[None, :] < send_count[0, 0][:, None]).astype(jnp.int32).reshape(n)
    refs, values = rating_pointer[0], rating_value[0]

    outgoing = pick_blocks(blocks, listed, live)
    incoming = lax.all_to_all(outgoing, "usr", split_axis=0, concat_axis=0, tiled=True)
    weights = make_weights(refs, values, n, height)
    packed, gathered = gram_terms(incoming.reshape(n * height, rank), refs, values, weights)
    share = packed.shape[0]
    draws = lax.dynamic_slice_in_dim(noise, lax.axis_index("grp") * share, share, 0)
    everyone = share_samples(solve_users(packed, draws, prior_prec, prior_shift))
    samples = lax.dynamic_index_in_dim(everyone, lax.axis_index("usr"), 0, keepdims=False)
    samples = samples.reshape(refs.shape[0], rank)
    stats = make_stats(gathered, everyone, listed, live, owned)
    return (samples, stats[None])


def solution(mesh):
    placed = (
        P("grp", "usr", None, None),
        P("grp", "usr", None, None),
        P("grp", "usr", None),
        P("grp", "usr", None),
        P("grp", "usr", None),
        P("usr", None),
        P(),
        P(),
    )
    return jax.shard_map(
        on_device,
        mesh=mesh,
        in_specs=placed,
        out_specs=(P("usr", None), P("grp", "usr", None, None)),
        check_vma=False,
    )
```
